256 devices in a mesh: section: 8 (over z_lo, core), ctx: 32 (over z_hi, x, y).
Axes of the slice: x: 4, y: 4, z: 8 (z_hi: 2, z_lo: 4; z = z_hi * 4 + z_lo), core: 2. Of those that a mesh axis runs over, the one named last changes fastest.
Arguments:
- section_input: bfloat16 [8, 1536, 8192], P('section', None, 'ctx'), may hold values from -6 to 6
- out_cotangent: bfloat16 [8, 1536, 2048], P('section', None, 'ctx'), may hold values from -96 to 96
- conv_weight: bfloat16 [8, 2, 1536, 640], P('section'), may hold values from -0.25 to 0.25
- norm_gain: float32 [8, 2, 1536], P('section'), may hold values from 0.1 to 1.9
Outputs:
- section_output: bfloat16 [8, 1536, 2048], P('section', None, 'ctx')
- input_grad: bfloat16 [8, 1536, 8192], P('section', None, 'ctx')
- weight_grad: float32 [8, 2, 1536, 640], P('section', None, 'ctx')
- gain_grad: float32 [8, 2, 1536], P('section', None, 'ctx')
The draws below stay inside these ranges and needn't reach their ends.
All inputs are finite; a program needn't handle non-finite values.
Results may differ from the reference program's by a relative error of at most 0.02.
Values may be sent and summed in bfloat16 or wider, within the bound.
A program may use at most 128 MiB of HBM per device.

```python
import jax
import jax.numpy as jnp
from jax import lax

C = 1536
GW = 128
SECTIONS = 8
POS = 8192
OUT_POS = 2048


def draw_out_cotangent(key, part):
    key = jax.random.fold_in(key, 11)
    key_base, key_chan, key_pos = jax.random.split(key, 3)
    shape = (SECTIONS, C, OUT_POS)
    section_pos = jnp.arange(SECTIONS, dtype=jnp.float32)[:, None, None]
    chan_pos = jnp.arange(C, dtype=jnp.float32)[None, :, None]
    section_factor = 3.0 ** (section_pos / max(SECTIONS - 1, 1) - 0.5)
    chan_factor = 3.0 ** (chan_pos / C - 0.5) * jnp.exp(jax.random.uniform(key_chan, (1, C, 1), jnp.float32, -0.6, 0.6))
    pos_factor = jnp.exp(jax.random.uniform(key_pos, (1, 1, OUT_POS), jnp.float32, -1.15, 1.15))
    base = jnp.clip(jax.random.normal(key_base, shape, jnp.float32), -4.0, 4.0)
    return (base * section_factor * chan_factor * pos_factor).astype(jnp.bfloat16)


def shard_levels(key, shape, shards, smallest, top_value):
    level, own = 1.0, jax.random.fold_in(key, 6)
    for position, blocks in shards:
        steps = jnp.exp(jax.random.uniform(jax.random.fold_in(own, position), (blocks,), jnp.float32, smallest / len(shards), top_value / len(shards)))
        level = level * jnp.repeat(steps, shape[position] // blocks).reshape([-1 if axis == position else 1 for axis in range(len(shape))])
    return level


def centred(key, shape, scale, bound, cuts=(), kind=jnp.bfloat16):
    values = jax.random.normal(key, shape, jnp.float32) * scale
    if len(cuts) > 0:
        values = shard_levels(key, shape, cuts, -0.22, 0.18) * values
    return jnp.clip(values, min=-bound, max=bound).astype(kind)


def setup_inputs(seed: int = 0) -> dict:
    arg_keys = jax.random.split(jax.random.key(seed), 5)
    return {
        "section_input": centred(arg_keys[0], (SECTIONS, C, POS), 1.0, 6.0, ((0, 8), (2, 32))),
        "out_cotangent": draw_out_cotangent(jax.random.fold_in(arg_keys[4], 71), 0),
        "conv_weight": centred(arg_keys[2], (SECTIONS, 2, C, 5 * GW), (5 * GW) ** -0.5, 0.25, ((0, 8),)),
        "norm_gain": jnp.clip(1.0 + 0.18 * jax.random.normal(arg_keys[3], (SECTIONS, 2, C), jnp.float32), 0.1, 1.9),
    }


def group_conv(padded, weight, length):
    channels = padded.shape[0]
    width = weight.shape[1] // 5
    groups = channels // width
    grouped = padded.reshape(groups, width, length + 4).astype(jnp.float32)
    stacked = jnp.concatenate([grouped[:, :, offset:offset + length] for offset in range(5)], axis=1)
    wgroup = weight.reshape(groups, width, 5 * width).astype(jnp.float32)
    result = jnp.einsum('gok,gkp->gop', wgroup, stacked)
    return (result.reshape(channels, length), stacked)

def forward_block(acts, weight, gain):
    channels, length = acts.shape
    halfway = channels // 2
    source = acts.astype(jnp.float32)
    inverse = 1.0 / jnp.sqrt(lax.optimization_barrier(jnp.mean(source * source, axis=0, keepdims=True)) + 1e-06)
    normed_raw = source * inverse
    normed = (normed_raw * gain[:, None]).astype(jnp.bfloat16)
    mirrored = normed[halfway:, ::-1]
    mixed = (normed[:halfway].astype(jnp.float32) + mirrored.astype(jnp.float32)).astype(jnp.bfloat16)
    inputs = jnp.concatenate([mixed, normed[halfway:]], axis=0)
    padded = jnp.pad(inputs, ((0, 0), (2, 2)))
    pre_act, stacked = group_conv(padded, weight, length)
    resid = source + jax.nn.gelu(pre_act)
    output = (0.5 * (resid[:, 0::2] + resid[:, 1::2])).astype(jnp.bfloat16)
    return (output, (normed_raw, inverse, pre_act, stacked))

def backward_block(grad_out, weight, gain, saved):
    normed_raw, inverse, pre_act, stacked = saved
    channels, length = normed_raw.shape
    halfway = channels // 2
    width = weight.shape[1] // 5
    groups = channels // width
    grad_res = jnp.repeat(grad_out, 2, axis=1) * 0.5
    unused, gelu_back = jax.vjp(jax.nn.gelu, pre_act)
    grad_pre = gelu_back(grad_res)[0].astype(jnp.bfloat16)
    pre_group = grad_pre.reshape(groups, width, length).astype(jnp.float32)
    wgrad = jnp.einsum('gop,gkp->gok', pre_group, stacked).reshape(channels, 5 * width)
    padded = jnp.pad(pre_group, ((0, 0), (0, 0), (2, 2)))
    shifted = jnp.stack([padded[:, :, 4 - offset:4 - offset + length] for offset in range(5)], axis=1)
    wfour = weight.reshape(groups, width, 5, width).astype(jnp.float32)
    grad_mixed = jnp.einsum('goki,gkop->gip', wfour, shifted).reshape(channels, length).astype(jnp.bfloat16)
    back = grad_mixed[:halfway, ::-1]
    grad_norm = jnp.concatenate([grad_mixed[:halfway].astype(jnp.float32), grad_mixed[halfway:].astype(jnp.float32) + back.astype(jnp.float32)], axis=0)
    ggrad = lax.optimization_barrier(jnp.sum(grad_norm * normed_raw, axis=1))
    scaled = grad_norm * gain[:, None]
    grad_in = (scaled - normed_raw * lax.optimization_barrier(jnp.mean(scaled * normed_raw, axis=0, keepdims=True))) * inverse + grad_res
    return (grad_in, wgrad, ggrad)

def one_section(items):
    acts, cotangent, weights, gains = items
    first, saved_one = forward_block(acts, weights[0], gains[0])
    second, saved_two = forward_block(first, weights[1], gains[1])
    grad_mid, wgrad_two, ggrad_two = backward_block(cotangent.astype(jnp.float32), weights[1], gains[1], saved_two)
    grad_in, wgrad_one, ggrad_one = backward_block(grad_mid, weights[0], gains[0], saved_one)
    return (second, grad_in.astype(jnp.bfloat16), jnp.stack([wgrad_one, wgrad_two]), jnp.stack([ggrad_one, ggrad_two]))

def reference(section_input, out_cotangent, conv_weight, norm_gain):
    second, grad_in, wgrads, ggrads = lax.map(one_section, (section_input, out_cotangent, conv_weight, norm_gain))
    total = jnp.sum(wgrads * wgrads) + jnp.sum(ggrads * ggrads)
    count = wgrads.size + ggrads.size
    factor = jnp.minimum(1.0, 1.0 / jnp.sqrt(total / count + 1e-06))
    return (second, grad_in, wgrads * factor, ggrads * factor)
```

```python
import jax
import jax.numpy as jnp
from jax import lax
from jax.experimental import pallas as pl
from jax.experimental.pallas import tpu as pltpu
from jax.sharding import PartitionSpec as P

MESH = pl.DeviceIdType.MESH
F32 = jnp.float32
BF16 = jnp.bfloat16
COUNT = 15753216.0


def reduce_kernel(w, dg, out, gout, ra, rb, pa, pb, qa, qb, sab, tz, gbuf, g1, g2, g3, sq, sq1, sq2,
                  ss1, rs1, ss2, rs2, ss3, rs3, sg, rg, sn, rn):
    sec = lax.axis_index("section")
    me = lax.axis_index("ctx")
    z = me // 16
    x = (me // 4) % 4
    y = me % 4
    plane = me % 16
    line = sec * 2 + z

    def at_x(d):
        return {"section": sec, "ctx": z * 16 + ((x + d) % 4) * 4 + y}

    def at_y(d):
        return {"section": sec, "ctx": z * 16 + x * 4 + (y + d) % 4}

    def at_z():
        return {"section": sec, "ctx": (1 - z) * 16 + plane}

    def at_plane(d):
        return {"section": sec, "ctx": z * 16 + (plane + d) % 16}

    def at_line(d):
        other = (line + d) % 16
        return {"section": other // 2, "ctx": (other % 2) * 16 + plane}

    def copy(src, dst, send, recv, device):
        return pltpu.make_async_remote_copy(
            src_ref=src, dst_ref=dst, send_sem=send, recv_sem=recv,
            device_id=device, device_id_type=MESH)

    barrier = pltpu.get_barrier_semaphore()
    for d in range(1, 16):
        pl.semaphore_signal(barrier, inc=1, device_id=at_plane(d), device_id_type=MESH)
        pl.semaphore_signal(barrier, inc=1, device_id=at_line(d), device_id_type=MESH)
    pl.semaphore_wait(barrier, 30)

    def first(b):
        cps = []
        for d in range(1, 4):
            cps.append(copy(w.at[b, 0, (x + d) % 4], ra.at[b, d - 1],
                            ss1.at[b, 0, d - 1], rs1.at[b, 0, d - 1], at_x(d)))
            cps.append(copy(w.at[b, 1, :, (y + d) % 4], rb.at[b, d - 1],
                            ss1.at[b, 1, d - 1], rs1.at[b, 1, d - 1], at_y(d)))
        return cps

    def second(b):
        cps = []
        for d in range(1, 4):
            cps.append(copy(pa.at[b, (y + d) % 4], qa.at[b, d - 1],
                            ss2.at[b, 0, d - 1], rs2.at[b, 0, d - 1], at_y(d)))
            cps.append(copy(pb.at[b, (x + d) % 4], qb.at[b, d - 1],
                            ss2.at[b, 1, d - 1], rs2.at[b, 1, d - 1], at_x(d)))
        return cps

    def third(b):
        return copy(sab.at[b, 1 - z], tz.at[b], ss3.at[b], rs3.at[b], at_z())

    def add_first(b):
        @pl.loop(0, 4)
        def _(k):
            a = w[b, 0, x, k].astype(F32)
            c = w[b, 1, k, y].astype(F32)
            for d in range(3):
                a += ra[b, d, k].astype(F32)
                c += rb[b, d, k].astype(F32)
            pa[b, k] = a.astype(BF16)
            pb[b, k] = c.astype(BF16)

    def add_second(b):
        a = pa[b, y].astype(F32)
        c = pb[b, x].astype(F32)
        for d in range(3):
            a += qa[b, d].astype(F32)
            c += qb[b, d].astype(F32)
        sab[b, 0] = a.astype(BF16)
        sab[b, 1] = c.astype(BF16)

    order = (1, 0)
    for b in order:
        for cp in first(b):
            cp.start()
    gbuf[0] = dg[...]
    gx = [copy(gbuf.at[0], g1.at[d - 1], sg.at[0, d - 1], rg.at[0, d - 1], at_x(d)) for d in range(1, 4)]
    for cp in gx:
        cp.start()
    for cp in gx:
        cp.wait()
    gbuf[1] = gbuf[0] + g1[0] + g1[1] + g1[2]
    gy = [copy(gbuf.at[1], g2.at[d - 1], sg.at[1, d - 1], rg.at[1, d - 1], at_y(d)) for d in range(1, 4)]
    for cp in gy:
        cp.start()
    for b in order:
        for cp in first(b):
            cp.wait()
        add_first(b)
        for cp in second(b):
            cp.start()
    for cp in gy:
        cp.wait()
    gbuf[2] = gbuf[1] + g2[0] + g2[1] + g2[2]
    gz = copy(gbuf.at[2], g3, sg.at[2, 0], rg.at[2, 0], at_z())
    gz.start()
    for b in order:
        for cp in second(b):
            cp.wait()
        add_second(b)
        third(b).start()
    gz.wait()
    total_g = gbuf[2] + g3[...]
    square = jnp.sum(total_g * total_g) * (1.0 / 32.0)
    for b in order:
        third(b).wait()
        full = sab[b, z].astype(F32) + tz[b].astype(F32)
        out[b] = full
        square += jnp.sum(full * full)
    sq[0] = jnp.full((8, 128), square, F32)
    near = [copy(sq.at[0], sq1.at[d - 1], sn.at[0, d - 1], rn.at[0, d - 1], at_plane(d)) for d in range(1, 16)]
    for cp in near:
        cp.start()
    for cp in near:
        cp.wait()
    sq[1] = sq[0] + jnp.sum(sq1[...], axis=0)
    far = [copy(sq.at[1], sq2.at[d - 1], sn.at[1, d - 1], rn.at[1, d - 1], at_line(d)) for d in range(1, 16)]
    for cp in far:
        cp.start()
    for cp in far:
        cp.wait()
    total = sq[1] + jnp.sum(sq2[...], axis=0)
    factor = jnp.minimum(1.0, lax.rsqrt(total / COUNT + 1e-06))[0:1, 0:1]
    for b in range(2):
        out[b] = out[b] * factor
    gout[...] = total_g * factor


def reduce_gradients(wgrads, ggrads):
    w = wgrads.astype(BF16).reshape(2, 2, 4, 4, 48, 640)
    dg = jnp.concatenate([ggrads.reshape(24, 128), jnp.zeros((8, 128), F32)])
    panel = pltpu.VMEM((2, 3, 4, 48, 640), BF16)
    dma = pltpu.SemaphoreType.DMA
    return pl.pallas_call(
        reduce_kernel,
        out_shape=(jax.ShapeDtypeStruct((2, 48, 640), F32), jax.ShapeDtypeStruct((32, 128), F32)),
        in_specs=[pl.BlockSpec(memory_space=pltpu.VMEM)] * 2,
        out_specs=[pl.BlockSpec(memory_space=pltpu.VMEM)] * 2,
        scratch_shapes=[
            panel, panel,
            pltpu.VMEM((2, 4, 48, 640), BF16), pltpu.VMEM((2, 4, 48, 640), BF16),
            pltpu.VMEM((2, 3, 48, 640), BF16), pltpu.VMEM((2, 3, 48, 640), BF16),
            pltpu.VMEM((2, 2, 48, 640), BF16), pltpu.VMEM((2, 48, 640), BF16),
            pltpu.VMEM((3, 32, 128), F32), pltpu.VMEM((3, 32, 128), F32),
            pltpu.VMEM((3, 32, 128), F32), pltpu.VMEM((32, 128), F32),
            pltpu.VMEM((2, 8, 128), F32), pltpu.VMEM((15, 8, 128), F32), pltpu.VMEM((15, 8, 128), F32),
            dma((2, 2, 3)), dma((2, 2, 3)), dma((2, 2, 3)), dma((2, 2, 3)), dma((2,)), dma((2,)),
            dma((3, 3)), dma((3, 3)), dma((2, 15)), dma((2, 15)),
        ],
        compiler_params=pltpu.CompilerParams(
            collective_id=0, has_side_effects=True, vmem_limit_bytes=48 << 20),
        name="reduce_gradients",
    )(w, dg)


def extended(x, sides, width):
    for axis, dim in sides:
        size, length = (lax.axis_size(axis), x.shape[dim])
        up = [(i, (i + 1) % size) for i in range(size - 1)]
        down = [(j, i) for i, j in up]
        last = lax.slice_in_dim(x, length - width, length, axis=dim)
        first = lax.slice_in_dim(x, 0, width, axis=dim)
        before = lax.ppermute(last, axis, up)
        after = lax.ppermute(first, axis, down)
        x = jnp.concatenate([before, x, after], axis=dim)
    return x


def mirror(panel):
    size = lax.axis_size("ctx")
    pairs = [(i, size - 1 - i) for i in range(size)]
    return lax.ppermute(panel[:, ::-1], "ctx", pairs)


def group_conv(padded, weight, length):
    channels = padded.shape[0]
    width = weight.shape[1] // 5
    groups = channels // width
    grouped = padded.reshape(groups, width, length + 4)
    stacked = jnp.concatenate(
        [grouped[:, :, offset : offset + length] for offset in range(5)], axis=1
    )
    wgroup = weight.reshape(groups, width, 5 * width)
    result = jnp.einsum("gok,gkp->gop", wgroup, stacked, preferred_element_type=jnp.float32)
    return (result.reshape(channels, length), stacked)


def forward_block(acts, weight, gain):
    channels, length = acts.shape
    halfway = channels // 2
    source = acts.astype(jnp.float32)
    inverse = lax.rsqrt(jnp.mean(source * source, axis=0, keepdims=True) + 1e-06)
    normed_raw = source * inverse
    normed = (normed_raw * gain[:, None]).astype(jnp.bfloat16)
    mirrored = mirror(normed[halfway:])
    mixed = (normed[:halfway].astype(jnp.float32) + mirrored.astype(jnp.float32)).astype(
        jnp.bfloat16
    )
    inputs = jnp.concatenate([mixed, normed[halfway:]], axis=0)
    padded = extended(inputs, (("ctx", 1),), 2)
    pre_act, stacked = group_conv(padded, weight, length)
    resid = source + jax.nn.gelu(pre_act)
    output = (0.5 * (resid[:, 0::2] + resid[:, 1::2])).astype(jnp.bfloat16)
    return (output, (normed_raw, inverse, pre_act, stacked))


def backward_block(grad_out, weight, gain, saved):
    normed_raw, inverse, pre_act, stacked = saved
    channels, length = normed_raw.shape
    halfway = channels // 2
    width = weight.shape[1] // 5
    groups = channels // width
    grad_res = jnp.repeat(grad_out, 2, axis=1) * 0.5
    unused, gelu_back = jax.vjp(jax.nn.gelu, pre_act)
    grad_pre = gelu_back(grad_res)[0].astype(jnp.bfloat16)
    pre_group = grad_pre.reshape(groups, width, length)
    wgrad = jnp.einsum(
        "gop,gkp->gok", pre_group, stacked, preferred_element_type=jnp.float32
    ).reshape(channels, 5 * width)
    padded = extended(grad_pre, (("ctx", 1),), 2).reshape(groups, width, length + 4)
    shifted = jnp.stack(
        [padded[:, :, 4 - offset : 4 - offset + length] for offset in range(5)], axis=1
    )
    wfour = weight.reshape(groups, width, 5, width)
    grad_mixed = (
        jnp.einsum("goki,gkop->gip", wfour, shifted, preferred_element_type=jnp.float32)
        .reshape(channels, length)
        .astype(jnp.bfloat16)
    )
    back = mirror(grad_mixed[:halfway])
    grad_norm = jnp.concatenate(
        [
            grad_mixed[:halfway].astype(jnp.float32),
            grad_mixed[halfway:].astype(jnp.float32) + back.astype(jnp.float32),
        ],
        axis=0,
    )
    ggrad = jnp.sum(grad_norm * normed_raw, axis=1)
    scaled = grad_norm * gain[:, None]
    grad_in = (
        scaled - normed_raw * jnp.mean(scaled * normed_raw, axis=0, keepdims=True)
    ) * inverse + grad_res
    return (grad_in, wgrad, ggrad)


def local(section_input, out_cotangent, conv_weight, norm_gain):
    acts = section_input[0]
    weights = conv_weight[0]
    gains = norm_gain[0]
    first, saved_one = forward_block(acts, weights[0], gains[0])
    second, saved_two = forward_block(first, weights[1], gains[1])
    grad_mid, wgrad_two, ggrad_two = backward_block(
        out_cotangent[0].astype(jnp.float32), weights[1], gains[1], saved_two
    )
    grad_in, wgrad_one, ggrad_one = backward_block(grad_mid, weights[0], gains[0], saved_one)
    wgrads = jnp.stack([wgrad_one, wgrad_two])
    ggrads = jnp.stack([ggrad_one, ggrad_two])
    wshare, gfull = reduce_gradients(wgrads, ggrads)
    me = lax.axis_index("ctx")
    gshare = lax.dynamic_slice(gfull[:24].reshape(2, 1536), (0, me * 48), (2, 48))
    return (
        second[None],
        grad_in.astype(jnp.bfloat16)[None],
        wshare[None],
        gshare[None],
    )


def solution(mesh):
    placed = (
        P("section", None, "ctx"),
        P("section", None, "ctx"),
        P("section", None, None, None),
        P("section", None, None),
    )
    return jax.shard_map(
        local,
        mesh=mesh,
        in_specs=placed,
        out_specs=(
            P("section", None, "ctx"),
            P("section", None, "ctx"),
            P("section", None, "ctx", None),
            P("section", None, "ctx"),
        ),
        check_vma=False,
    )
```

```python
import jax
import jax.numpy as jnp
from jax import lax
from jax.experimental import pallas as pl
from jax.experimental.pallas import tpu as pltpu
from jax.sharding import PartitionSpec as P

MESH = pl.DeviceIdType.MESH
F32 = jnp.float32
BF16 = jnp.bfloat16
COUNT = 15753216.0
CHANNELS = 1536.0
NT = (((1,), (1,)), ((), ()))
TN = (((0,), (0,)), ((), ()))


def iota(shape, dim):
    return lax.broadcasted_iota(jnp.int32, shape, dim)


def dot(a, b, dims=(((1,), (0,)), ((), ()))):
    return lax.dot_general(a, b, dims, preferred_element_type=F32)


def split_dot(a, b):
    high = a.astype(BF16)
    low = (a - high.astype(F32)).astype(BF16)
    return dot(high, b) + dot(low, b)


def reversal(length):
    shape = (length, length)
    return (iota(shape, 0) + iota(shape, 1) == length - 1).astype(F32).astype(BF16)


def pooling(length):
    shape = (length, length // 2)
    return jnp.where(iota(shape, 0) // 2 == iota(shape, 1), 0.5, 0.0).astype(BF16)


def spreading(length):
    shape = (length // 2, length)
    return jnp.where(iota(shape, 0) == iota(shape, 1) // 2, 0.5, 0.0).astype(BF16)


def edge_pick(slot, length):
    shape = (32, length)
    row = iota(shape, 0)
    j = row % 16 - 2 * slot
    target = j + jnp.where(row >= 16, length - 2, 0)
    hit = jnp.logical_and(jnp.logical_and(j >= 0, j < 2), iota(shape, 1) == target)
    return jnp.where(hit, 1.0, 0.0).astype(BF16)


def halo_place(slot, rows):
    shape = (rows, 128)
    row = iota(shape, 0)
    block = row // 16
    j = row % 16 - 2 * slot
    straight = jnp.where(block == 0, j, 126 + j)
    turned = jnp.where(block == 2, 1 - j, 127 - j)
    target = jnp.where(block < 2, straight, turned)
    hit = jnp.logical_and(jnp.logical_and(j >= 0, j < 2), iota(shape, 1) == target)
    return jnp.where(hit, 1.0, 0.0).astype(BF16)


def as_row(column):
    shape = (128, 128)
    return jnp.sum(jnp.where(iota(shape, 0) == iota(shape, 1), column, 0.0), axis=0, keepdims=True)


def fold(value):
    rows, length = value.shape
    return jnp.sum(value.reshape(rows // 8, 8, length), axis=0)


def gelu_parts(y):
    c0 = 0.7978845608028654
    square = y * y
    t = jnp.tanh(c0 * (y + 0.044715 * (square * y)))
    cdf = 0.5 * (1.0 + t)
    slope = cdf + 0.5 * y * (1.0 - t * t) * (c0 * (1.0 + 0.134145 * square))
    return y * cdf, slope


def kernel(h0, cot, wt_in, gain, sec_out, ig_out, out, gout,
           gcol, wtr, nb0, nb1, h1, s0, s1, gp0, dr0, dr1, dyb0, dyb1, dn0, dn1, dzs0, dzs1, nrev,
           rc0, rc1, rc2, rc3, esend, eright, eleft, eright_m, eleft_m, dgb,
           w, ra, rb, pa, pb, qa, qb, sab, tz, gbuf, g1, g2, g3, sq, sq1, sq2,
           psend, precv, esem, ersem,
           ss1, rs1, ss2, rs2, ss3, rs3, sg, rg, sn, rn):
    sec = lax.axis_index("section")
    me = lax.axis_index("ctx")
    z = me // 16
    x = (me // 4) % 4
    y = me % 4
    plane = me % 16
    line = sec * 2 + z
    has_left = me > 0
    has_right = me < 31
    not_15 = jnp.logical_and(has_right, me != 15)
    not_16 = jnp.logical_and(has_left, me != 16)

    def ctx(index):
        return {"section": sec, "ctx": index}

    def at_x(d):
        return ctx(z * 16 + ((x + d) % 4) * 4 + y)

    def at_y(d):
        return ctx(z * 16 + x * 4 + (y + d) % 4)

    def at_z():
        return ctx((1 - z) * 16 + plane)

    def at_plane(d):
        return ctx(z * 16 + (plane + d) % 16)

    def at_line(d):
        other = (line + d) % 16
        return {"section": other // 2, "ctx": (other % 2) * 16 + plane}

    to_mirror = ctx(31 - me)
    to_left = ctx((me + 31) % 32)
    to_right = ctx((me + 1) % 32)
    to_right_m = ctx((62 - me) % 32)
    to_left_m = ctx((32 - me) % 32)

    def copy(src, dst, send, recv, device):
        return pltpu.make_async_remote_copy(
            src_ref=src, dst_ref=dst, send_sem=send, recv_sem=recv,
            device_id=device, device_id_type=MESH)

    eright[...] = jnp.zeros_like(eright)
    eleft[...] = jnp.zeros_like(eleft)
    eright_m[...] = jnp.zeros_like(eright_m)
    eleft_m[...] = jnp.zeros_like(eleft_m)
    dgb[...] = jnp.zeros_like(dgb)

    barrier = pltpu.get_barrier_semaphore()

    def greet(device):
        pl.semaphore_signal(barrier, inc=1, device_id=device, device_id_type=MESH)

    greet(to_mirror)
    for d in range(1, 16):
        greet(at_plane(d))
        greet(at_line(d))

    @pl.when(has_left)
    def _():
        greet(to_left)

    @pl.when(has_right)
    def _():
        greet(to_right)

    @pl.when(not_15)
    def _():
        greet(to_right_m)

    @pl.when(not_16)
    def _():
        greet(to_left_m)

    def edge_copies(s):
        left = copy(esend.at[s, 0], eright.at[s], esem.at[s, 0], ersem.at[s, 0], to_left)
        right = copy(esend.at[s, 1], eleft.at[s], esem.at[s, 1], ersem.at[s, 1], to_right)
        right_m = left_m = None
        if s < 2:
            right_m = copy(esend.at[s, 1, 1], eright_m.at[s], esem.at[s, 2], ersem.at[s, 2], to_right_m)
            left_m = copy(esend.at[s, 0, 1], eleft_m.at[s], esem.at[s, 3], ersem.at[s, 3], to_left_m)
        return left, right, right_m, left_m

    def edges_start(s):
        left, right, right_m, left_m = edge_copies(s)
        pl.when(has_left)(left.start)
        pl.when(has_right)(right.start)
        if s < 2:
            pl.when(not_15)(right_m.start)
            pl.when(not_16)(left_m.start)

            @pl.when(me == 15)
            def _():
                eright_m[s] = esend[s, 1, 1]

            @pl.when(me == 16)
            def _():
                eleft_m[s] = esend[s, 0, 1]

    def edges_wait(s):
        left, right, right_m, left_m = edge_copies(s)
        pl.when(has_left)(left.wait_send)
        pl.when(has_right)(left.wait_recv)
        pl.when(has_right)(right.wait_send)
        pl.when(has_left)(right.wait_recv)
        if s < 2:
            pl.when(not_15)(right_m.wait)
            pl.when(not_16)(left_m.wait)

    def edges_store(s, half, value):
        esend[s, 0, half] = value[0:16].astype(BF16)
        esend[s, 1, half] = value[16:32].astype(BF16)

    def halo(s, half, slot, mirrored):
        parts = [eright[s, half], eleft[s, half]]
        if mirrored:
            parts += [eright_m[s], eleft_m[s]]
        return dot(jnp.concatenate(parts, axis=0), halo_place(slot, 16 * len(parts)), TN)

    def panel(step, g):
        src, dst = ((nb0.at[g + 6], rc0.at[g]), (nb1.at[g + 6], rc1.at[g]),
                    (dzs1.at[g], rc2.at[g]), (dzs0.at[g], rc3.at[g]))[step]
        return copy(src, dst, psend.at[step, g], precv.at[step, g], to_mirror)

    def shifted(value, tail, sign, store):
        length = value.shape[1]
        wide = jnp.concatenate([value, tail], axis=1)
        for k in range(5):
            shift = (sign * (2 - k)) % (length + 128)
            turned = wide if shift == 0 else pltpu.roll(wide, shift, 1)
            store(k, turned[:, :length].astype(BF16))

    @pl.loop(0, 24)
    def _(i):
        shape = (128, 128)
        column = jnp.sum(
            jnp.where(iota(shape, 0) == iota(shape, 1), gain[pl.ds(i, 1), :], 0.0), axis=1, keepdims=True)
        gcol[i] = jnp.broadcast_to(column, shape)

    def inverse_of(total):
        return lax.rsqrt(jnp.sum(total, axis=0, keepdims=True) / CHANNELS + 1e-06)

    def norm(block, acts, inverse, length, target, s):
        g_wide = length // 128
        for half in (1, 0):
            def body(i, edge):
                g = half * 6 + i
                column = gcol[block * 12 + g]
                wide = jnp.concatenate([column] * g_wide, axis=1)
                value = ((acts[g].astype(F32) * inverse) * wide).astype(BF16)
                target[g] = value
                return edge + dot(edge_pick(i, length), value, NT)
            edges_store(s, half, lax.fori_loop(0, 6, body, jnp.zeros((32, 128), F32)))

    total0 = lax.fori_loop(
        0, 12, lambda g, t: t + fold(jnp.square(h0[g].astype(F32))), jnp.zeros((8, 256), F32))
    inv0 = inverse_of(total0)
    norm(0, h0, inv0, 256, nb0, 0)

    pl.semaphore_wait(
        barrier, 31 + has_left.astype(jnp.int32) + has_right.astype(jnp.int32)
        + not_15.astype(jnp.int32) + not_16.astype(jnp.int32))
    edges_start(0)

    @pl.loop(0, 6)
    def _(g):
        panel(0, g).start()

    @pl.loop(0, 12)
    def _(g):
        for b in range(2):
            for k in range(5):
                wtr[b, g, :, k * 128:(k + 1) * 128] = wt_in[b, g, :, k * 128:(k + 1) * 128].T

    edges_wait(0)

    def conv0(g, value, tail):
        def store(k, part):
            s0[g, k * 128:(k + 1) * 128, :] = part
        shifted(value, tail, 1, store)
        act, slope = gelu_parts(dot(wt_in[0, g], s0[g]))
        gp0[g] = slope
        res = h0[g].astype(F32) + act
        pooled = split_dot(res, pooling(256)).astype(BF16)
        h1[g] = pooled
        return fold(jnp.square(pooled.astype(F32)))

    def hi0(i, t):
        g = i + 6
        return t + conv0(g, nb0[g].astype(F32), halo(0, 1, i, False))

    def lo0(g, t):
        panel(0, g).wait()
        turned = dot(rc0[g], reversal(256))
        nrev[g] = turned.astype(BF16)
        return t + conv0(g, nb0[g].astype(F32) + turned, halo(0, 0, g, True))

    total1 = lax.fori_loop(0, 6, hi0, jnp.zeros((8, 128), F32))
    total1 = lax.fori_loop(0, 6, lo0, total1)
    inv1 = inverse_of(total1)
    norm(1, h1, inv1, 128, nb1, 1)
    edges_start(1)

    @pl.loop(0, 6)
    def _(g):
        panel(1, g).start()

    edges_wait(1)

    def conv1(g, slot, value, tail):
        def store(k, part):
            s1[g, k * 128:(k + 1) * 128, :] = part
        shifted(value, tail, 1, store)
        act, slope = gelu_parts(dot(wt_in[1, g], s1[g]))
        res = h1[g].astype(F32) + act
        sec_out[g] = split_dot(res, pooling(128)).astype(BF16)
        dr = dot(cot[g], spreading(128))
        dr1[g] = dr
        dy = (dr * slope).astype(BF16)
        dyb1[g] = dy
        return dot(edge_pick(slot, 128), dy, NT)

    def hi1(i, e):
        g = i + 6
        return e + conv1(g, i, nb1[g].astype(F32), halo(1, 1, i, False))

    def lo1(g, e):
        panel(1, g).wait()
        turned = dot(rc1[g], reversal(128))
        return e + conv1(g, g, nb1[g].astype(F32) + turned, halo(1, 0, g, True))

    edges_store(2, 1, lax.fori_loop(0, 6, hi1, jnp.zeros((32, 128), F32)))
    edges_store(2, 0, lax.fori_loop(0, 6, lo1, jnp.zeros((32, 128), F32)))
    edges_start(2)

    def weight_grads(b, dyb, stacks):
        @pl.loop(0, 12)
        def _(i):
            g = (i + 6) % 12
            grad = dot(dyb[g], stacks[g], NT).astype(BF16)
            for j in range(8):
                piece = g * 8 + j
                block = piece // 3
                w[b, block // 16, (block // 4) % 4, block % 4, piece % 3] = grad[j * 16:(j + 1) * 16]

    def first(b):
        cps = []
        for d in range(1, 4):
            cps.append(copy(w.at[b, 1, :, (y + d) % 4], rb.at[b, d - 1],
                            ss1.at[b, 1, d - 1], rs1.at[b, 1, d - 1], at_y(d)))
            cps.append(copy(w.at[b, 0, (x + d) % 4], ra.at[b, d - 1],
                            ss1.at[b, 0, d - 1], rs1.at[b, 0, d - 1], at_x(d)))
        return cps

    def second(b):
        cps = []
        for d in range(1, 4):
            cps.append(copy(pa.at[b, (y + d) % 4], qa.at[b, d - 1],
                            ss2.at[b, 0, d - 1], rs2.at[b, 0, d - 1], at_y(d)))
            cps.append(copy(pb.at[b, (x + d) % 4], qb.at[b, d - 1],
                            ss2.at[b, 1, d - 1], rs2.at[b, 1, d - 1], at_x(d)))
        return cps

    def third(b):
        return copy(sab.at[b, 1 - z], tz.at[b], ss3.at[b], rs3.at[b], at_z())

    def add_first(b):
        for cp in first(b):
            cp.wait()

        @pl.loop(0, 4)
        def _(k):
            a = w[b, 0, x, k].astype(F32)
            c = w[b, 1, k, y].astype(F32)
            for d in range(3):
                a += ra[b, d, k].astype(F32)
                c += rb[b, d, k].astype(F32)
            pa[b, k] = a.astype(BF16)
            pb[b, k] = c.astype(BF16)
        for cp in second(b):
            cp.start()

    def add_second(b):
        for cp in second(b):
            cp.wait()
        a = pa[b, y].astype(F32)
        c = pb[b, x].astype(F32)
        for d in range(3):
            a += qa[b, d].astype(F32)
            c += qb[b, d].astype(F32)
        sab[b, 0] = a.astype(BF16)
        sab[b, 1] = c.astype(BF16)
        third(b).start()

    weight_grads(1, dyb1, s1)
    for cp in first(1):
        cp.start()
    edges_wait(2)

    def back(b, g, slot, half, s, dyb, length):
        parts = [None] * 5

        def store(k, part):
            parts[k] = part
        shifted(dyb[g].astype(F32), halo(s, half, slot, False), -1, store)
        return dot(wtr[b, g], jnp.concatenate(parts, axis=0)).astype(BF16)

    def scaled_sum(dn, xhat, row, length):
        weighted = dn * xhat
        column = jnp.sum(weighted, axis=1, keepdims=True)
        return fold(weighted * jnp.concatenate([gcol[row]] * (length // 128), axis=1)), as_row(column)

    def lo1_back(g, q):
        dz = back(1, g, g, 0, 2, dyb1, 128)
        dzs1[g] = dz
        panel(2, g).start()
        dn = dz.astype(F32)
        dn1[g] = dn
        part, row = scaled_sum(dn, h1[g].astype(F32) * inv1, 12 + g, 128)
        dgb[pl.ds(12 + g, 1), :] = row
        return q + part

    q1 = lax.fori_loop(0, 6, lo1_back, jnp.zeros((8, 128), F32))

    @pl.loop(6, 12)
    def _(g):
        dn1[g] = back(1, g, g - 6, 1, 2, dyb1, 128).astype(F32)

    def hi1_back(i, q):
        g = i + 6
        panel(2, i).wait()
        dn = dn1[g] + dot(rc2[i], reversal(128))
        dn1[g] = dn
        part, row = scaled_sum(dn, h1[g].astype(F32) * inv1, 12 + g, 128)
        dgb[pl.ds(12 + g, 1), :] = row
        return q + part

    q1 = lax.fori_loop(0, 6, hi1_back, q1)
    mean1 = jnp.sum(q1, axis=0, keepdims=True) / CHANNELS

    for half in (1, 0):
        def step(i, e):
            g = half * 6 + i
            xhat = h1[g].astype(F32) * inv1
            dh = (dn1[g] * gcol[12 + g] - xhat * mean1) * inv1 + dr1[g]
            dr = split_dot(dh, spreading(256))
            dr0[g] = dr
            dy = (dr * gp0[g]).astype(BF16)
            dyb0[g] = dy
            return e + dot(edge_pick(i, 256), dy, NT)
        edges_store(3, half, lax.fori_loop(0, 6, step, jnp.zeros((32, 128), F32)))
    edges_start(3)
    weight_grads(0, dyb0, s0)
    for cp in first(0):
        cp.start()
    add_first(1)
    edges_wait(3)

    def lo0_back(g, q):
        dz = back(0, g, g, 0, 3, dyb0, 256)
        dzs0[g] = dz
        panel(3, g).start()
        dn = dz.astype(F32)
        dn0[g] = dn
        part, row = scaled_sum(dn, h0[g].astype(F32) * inv0, g, 256)
        dgb[pl.ds(g, 1), :] = row
        column = jnp.sum(dn * nrev[g].astype(F32), axis=1, keepdims=True) / gcol[6 + g]
        dgb[pl.ds(6 + g, 1), :] = as_row(column)
        return q + part

    q0 = lax.fori_loop(0, 6, lo0_back, jnp.zeros((8, 256), F32))

    @pl.loop(6, 12)
    def _(g):
        dn = back(0, g, g - 6, 1, 3, dyb0, 256).astype(F32)
        dn0[g] = dn
        column = jnp.sum(dn * (h0[g].astype(F32) * inv0), axis=1, keepdims=True)
        dgb[pl.ds(g, 1), :] += as_row(column)

    gbuf[0] = dgb[...]
    gx = [copy(gbuf.at[0], g1.at[d - 1], sg.at[0, d - 1], rg.at[0, d - 1], at_x(d)) for d in range(1, 4)]
    gy = [copy(gbuf.at[1], g2.at[d - 1], sg.at[1, d - 1], rg.at[1, d - 1], at_y(d)) for d in range(1, 4)]
    gz = copy(gbuf.at[2], g3, sg.at[2, 0], rg.at[2, 0], at_z())
    for cp in gx:
        cp.start()
    add_second(1)
    add_first(0)
    for cp in gx:
        cp.wait()
    gbuf[1] = gbuf[0] + g1[0] + g1[1] + g1[2]
    for cp in gy:
        cp.start()
    add_second(0)
    for cp in gy:
        cp.wait()
    gbuf[2] = gbuf[1] + g2[0] + g2[1] + g2[2]
    gz.start()

    def hi0_back(i, q):
        g = i + 6
        panel(3, i).wait()
        dn = dn0[g] + dot(rc3[i], reversal(256))
        dn0[g] = dn
        xhat = h0[g].astype(F32) * inv0
        return q + fold(dn * xhat * jnp.concatenate([gcol[g]] * 2, axis=1))

    q0 = lax.fori_loop(0, 6, hi0_back, q0)
    mean0 = jnp.sum(q0, axis=0, keepdims=True) / CHANNELS

    gz.wait()
    total_g = gbuf[2] + g3[...]
    square = jnp.sum(total_g * total_g) * (1.0 / 32.0)
    for b in (1, 0):
        third(b).wait()
        full = sab[b, z].astype(F32) + tz[b].astype(F32)
        out[b] = full
        square += jnp.sum(full * full)
    sq[0] = jnp.full((8, 128), square, F32)
    near = [copy(sq.at[0], sq1.at[d - 1], sn.at[0, d - 1], rn.at[0, d - 1], at_plane(d)) for d in range(1, 16)]
    for cp in near:
        cp.start()

    @pl.loop(0, 12)
    def _(g):
        xhat = h0[g].astype(F32) * inv0
        wide = jnp.concatenate([gcol[g]] * 2, axis=1)
        ig_out[g] = ((dn0[g] * wide - xhat * mean0) * inv0 + dr0[g]).astype(BF16)

    for cp in near:
        cp.wait()
    sq[1] = sq[0] + jnp.sum(sq1[...], axis=0)
    far = [copy(sq.at[1], sq2.at[d - 1], sn.at[1, d - 1], rn.at[1, d - 1], at_line(d)) for d in range(1, 16)]
    for cp in far:
        cp.start()
    for cp in far:
        cp.wait()
    total = sq[1] + jnp.sum(sq2[...], axis=0)
    factor = jnp.minimum(1.0, lax.rsqrt(total / COUNT + 1e-06))[0:1, 0:1]
    for b in range(2):
        out[b] = out[b] * factor
    gout[...] = total_g * factor


def local(section_input, out_cotangent, conv_weight, norm_gain):
    h0 = section_input.reshape(12, 128, 256)
    cot = out_cotangent.reshape(12, 128, 64)
    weights = conv_weight.reshape(2, 12, 128, 640)
    gain = norm_gain.reshape(24, 128)
    dma = pltpu.SemaphoreType.DMA

    def vm(shape, kind=BF16):
        return pltpu.VMEM(shape, kind)

    second, grad_in, wshare, gfull = pl.pallas_call(
        kernel,
        out_shape=(
            jax.ShapeDtypeStruct((12, 128, 64), BF16),
            jax.ShapeDtypeStruct((12, 128, 256), BF16),
            jax.ShapeDtypeStruct((2, 3, 16, 640), F32),
            jax.ShapeDtypeStruct((32, 128), F32),
        ),
        in_specs=[pl.BlockSpec(memory_space=pltpu.VMEM)] * 4,
        out_specs=[pl.BlockSpec(memory_space=pltpu.VMEM)] * 4,
        scratch_shapes=[
            vm((24, 128, 128), F32), vm((2, 12, 128, 640)),
            vm((12, 128, 256)), vm((12, 128, 128)), vm((12, 128, 128)),
            vm((12, 640, 256)), vm((12, 640, 128)),
            vm((12, 128, 256), F32), vm((12, 128, 256), F32), vm((12, 128, 128), F32),
            vm((12, 128, 256)), vm((12, 128, 128)),
            vm((12, 128, 256), F32), vm((12, 128, 128), F32),
            vm((6, 128, 256)), vm((6, 128, 128)), vm((6, 128, 256)),
            vm((6, 128, 256)), vm((6, 128, 128)), vm((6, 128, 128)), vm((6, 128, 256)),
            vm((4, 2, 2, 16, 128)), vm((4, 2, 16, 128)), vm((4, 2, 16, 128)),
            vm((2, 16, 128)), vm((2, 16, 128)), vm((32, 128), F32),
            vm((2, 2, 4, 4, 3, 16, 640)), vm((2, 3, 4, 3, 16, 640)), vm((2, 3, 4, 3, 16, 640)),
            vm((2, 4, 3, 16, 640)), vm((2, 4, 3, 16, 640)),
            vm((2, 3, 3, 16, 640)), vm((2, 3, 3, 16, 640)),
            vm((2, 2, 3, 16, 640)), vm((2, 3, 16, 640)),
            vm((3, 32, 128), F32), vm((3, 32, 128), F32), vm((3, 32, 128), F32), vm((32, 128), F32),
            vm((2, 8, 128), F32), vm((15, 8, 128), F32), vm((15, 8, 128), F32),
            dma((4, 6)), dma((4, 6)), dma((4, 4)), dma((4, 4)),
            dma((2, 2, 3)), dma((2, 2, 3)), dma((2, 2, 3)), dma((2, 2, 3)), dma((2,)), dma((2,)),
            dma((3, 3)), dma((3, 3)), dma((2, 15)), dma((2, 15)),
        ],
        compiler_params=pltpu.CompilerParams(
            collective_id=0, has_side_effects=True, vmem_limit_bytes=56 << 20),
        name="tower",
    )(h0, cot, weights, gain)
    me = lax.axis_index("ctx")
    gshare = lax.dynamic_slice(gfull[:24].reshape(2, 1536), (0, me * 48), (2, 48))
    return (
        second.reshape(1, 1536, 64),
        grad_in.reshape(1, 1536, 256),
        wshare.reshape(1, 2, 48, 640),
        gshare[None],
    )


def solution(mesh):
    placed = (
        P("section", None, "ctx"),
        P("section", None, "ctx"),
        P("section", None, None, None),
        P("section", None, None),
    )
    return jax.shard_map(
        local,
        mesh=mesh,
        in_specs=placed,
        out_specs=(
            P("section", None, "ctx"),
            P("section", None, "ctx"),
            P("section", None, "ctx", None),
            P("section", None, "ctx"),
        ),
        check_vma=False,
    )
```

```python
import jax
import jax.numpy as jnp
from jax import lax
from jax.experimental import pallas as pl
from jax.experimental.pallas import tpu as pltpu
from jax.sharding import PartitionSpec as P

MESH = pl.DeviceIdType.MESH
F32 = jnp.float32
BF16 = jnp.bfloat16
COUNT = 15753216.0
CHANNELS = 1536.0
PER = 6
NT = (((1,), (1,)), ((), ()))
TN = (((0,), (0,)), ((), ()))


def iota(shape, dim):
    return lax.broadcasted_iota(jnp.int32, shape, dim)


def dot(a, b, dims=(((1,), (0,)), ((), ()))):
    return lax.dot_general(a, b, dims, preferred_element_type=F32)


def two_terms(a):
    high = a.astype(BF16)
    return high, (a - high.astype(F32)).astype(BF16)


def reversal(length):
    shape = (length, length)
    return jnp.where(iota(shape, 0) + iota(shape, 1) == length - 1, 1.0, 0.0).astype(BF16)


def spreading(length):
    shape = (length // 2, length)
    return jnp.where(iota(shape, 0) == iota(shape, 1) // 2, 0.5, 0.0).astype(BF16)


def edge_pick(slot, length):
    shape = (32, length)
    row = iota(shape, 0)
    j = row % 16 - 2 * slot
    target = j + jnp.where(row >= 16, length - 2, 0)
    hit = jnp.logical_and(jnp.logical_and(j >= 0, j < 2), iota(shape, 1) == target)
    return jnp.where(hit, 1.0, 0.0).astype(BF16)


def halo_place(slot):
    shape = (64, 128)
    row = iota(shape, 0)
    block = row // 16
    j = row % 16 - 2 * slot
    straight = jnp.where(block == 0, j, 126 + j)
    turned = jnp.where(block == 2, 1 - j, 127 - j)
    target = jnp.where(block < 2, straight, turned)
    hit = jnp.logical_and(jnp.logical_and(j >= 0, j < 2), iota(shape, 1) == target)
    return jnp.where(hit, 1.0, 0.0).astype(BF16)


def wide(column, length):
    return column if length == 128 else jnp.concatenate([column] * (length // 128), axis=1)


def run(low, high, body, carry, per):
    if per >= high - low:
        for i in range(low, high):
            carry = body(i, carry)
        return carry

    def several(k, c):
        for u in range(per):
            c = body(low + k * per + u, c)
        return c
    return lax.fori_loop(0, (high - low) // per, several, carry)


def as_row(column):
    shape = (128, 128)
    return jnp.sum(jnp.where(iota(shape, 0) == iota(shape, 1), column, 0.0), axis=0, keepdims=True)


def fold(value):
    rows, length = value.shape
    return jnp.sum(value.reshape(rows // 8, 8, length), axis=0)


def gelu_parts(y):
    c0 = 0.7978845608028654
    square = y * y
    t = jnp.tanh(c0 * (y + 0.044715 * (square * y)))
    cdf = 0.5 * (1.0 + t)
    slope = cdf + 0.5 * y * (1.0 - t * t) * (c0 * (1.0 + 0.134145 * square))
    return y * cdf, slope


def kernel(h0_hbm, cot, wt_hbm, gain, sec_hbm, ig_hbm, out, gout,
           h0, wt_in, secb, igb, rev, spread, pick0, pick1, place, iv0s, iv1s, iv0r, iv1r, gfull,
           gcol, wtr, nb0, nb1, h1, s0, s1, gp0, dr0, dr1, dyb0, dyb1, dn0, dn1, dzs0, dzs1, nrev,
           rc0, rc1, rc2, rc3, esend, eright, eleft, eright_m, eleft_m, dgb,
           w, rr, pp, qq, sab, tz, nrev1, qs, qr, gbuf, g1, g2, g3, sq, sq1, sq2,
           psend, precv, esem, ersem, ivsem, ivrsem, lsem, qsem, qrsem,
           ss1, rs1, ss2, rs2, ss3, rs3, sg, rg, sn, rn):
    sec = lax.axis_index("section")
    me = lax.axis_index("ctx")
    z = me // 16
    x = (me // 4) % 4
    y = me % 4
    plane = me % 16
    line = sec * 2 + z
    has_left = me > 0
    has_right = me < 31
    not_15 = jnp.logical_and(has_right, me != 15)
    not_16 = jnp.logical_and(has_left, me != 16)

    def ctx(index):
        return {"section": sec, "ctx": index}

    def at_x(d):
        return ctx(z * 16 + ((x + d) % 4) * 4 + y)

    def at_y(d):
        return ctx(z * 16 + x * 4 + (y + d) % 4)

    def at_z():
        return ctx((1 - z) * 16 + plane)

    def at_plane(d):
        return ctx(z * 16 + (plane + d) % 16)

    def at_line(d):
        other = (line + d) % 16
        return {"section": other // 2, "ctx": (other % 2) * 16 + plane}

    to_mirror = ctx(31 - me)
    to_left = ctx((me + 31) % 32)
    to_right = ctx((me + 1) % 32)
    to_right_m = ctx((62 - me) % 32)
    to_left_m = ctx((32 - me) % 32)

    def copy(src, dst, send, recv, device):
        return pltpu.make_async_remote_copy(
            src_ref=src, dst_ref=dst, send_sem=send, recv_sem=recv,
            device_id=device, device_id_type=MESH)

    eright[...] = jnp.zeros_like(eright)
    eleft[...] = jnp.zeros_like(eleft)
    eright_m[...] = jnp.zeros_like(eright_m)
    eleft_m[...] = jnp.zeros_like(eleft_m)
    dgb[...] = jnp.zeros_like(dgb)

    barrier = pltpu.get_barrier_semaphore()

    def greet(device):
        pl.semaphore_signal(barrier, inc=1, device_id=device, device_id_type=MESH)

    greet(to_mirror)

    @pl.when(not_15)
    def _():
        greet(to_right_m)

    @pl.when(not_16)
    def _():
        greet(to_left_m)

    for d in (8, 7, 9, 6, 10, 5, 11, 4, 12, 3, 13, 2, 14, 1, 15):
        greet(at_line(d))

    @pl.when(has_left)
    def _():
        greet(to_left)

    @pl.when(has_right)
    def _():
        greet(to_right)

    for d in range(1, 16):
        greet(at_plane(d))

    h0_load = pltpu.make_async_copy(h0_hbm, h0, lsem.at[0])
    w_load = pltpu.make_async_copy(wt_hbm, wt_in, lsem.at[1])
    h0_load.start()
    w_load.start()

    for b in range(2):
        value = jnp.broadcast_to(gain[b:b + 1, :], (16, 1536))
        top = value.astype(BF16).astype(F32)
        middle = (value - top).astype(BF16).astype(F32)
        rest = value - top - middle
        row = iota((16, 1536), 0)
        terms = jnp.where(row == 0, top, jnp.where(row == 1, middle, jnp.where(row == 2, rest, 0.0)))
        terms = terms.astype(BF16)
        ones = jnp.ones((16, 128), BF16)
        for g in range(12):
            gcol[b * 12 + g] = dot(terms[:, g * 128:(g + 1) * 128], ones, TN)
    spread[...] = spreading(256)

    pl.semaphore_wait(
        barrier, 31 + has_left.astype(jnp.int32) + has_right.astype(jnp.int32)
        + not_15.astype(jnp.int32) + not_16.astype(jnp.int32))

    def half_copies(s, half):
        left = copy(esend.at[s, 0, half], eright.at[s, half], esem.at[s, 2 * half], ersem.at[s, 2 * half], to_left)
        right = copy(esend.at[s, 1, half], eleft.at[s, half],
                     esem.at[s, 2 * half + 1], ersem.at[s, 2 * half + 1], to_right)
        return left, right

    def half_start(s, half):
        left, right = half_copies(s, half)
        pl.when(has_left)(left.start)
        pl.when(has_right)(right.start)

    def near_wait(left, right):
        pl.when(has_left)(left.wait_send)
        pl.when(has_right)(left.wait_recv)
        pl.when(has_right)(right.wait_send)
        pl.when(has_left)(right.wait_recv)

    def half_wait(s, half):
        near_wait(*half_copies(s, half))

    def edge_copies(s):
        left = copy(esend.at[s, 0], eright.at[s], esem.at[s, 0], ersem.at[s, 0], to_left)
        right = copy(esend.at[s, 1], eleft.at[s], esem.at[s, 1], ersem.at[s, 1], to_right)
        right_m = left_m = None
        if s < 2:
            right_m = copy(esend.at[s, 1, 1], eright_m.at[s], esem.at[s, 2], ersem.at[s, 2], to_right_m)
            left_m = copy(esend.at[s, 0, 1], eleft_m.at[s], esem.at[s, 3], ersem.at[s, 3], to_left_m)
        return left, right, right_m, left_m

    def edges_start(s):
        left, right, right_m, left_m = edge_copies(s)
        pl.when(has_left)(left.start)
        pl.when(has_right)(right.start)
        if s < 2:
            pl.when(not_15)(right_m.start)
            pl.when(not_16)(left_m.start)

            @pl.when(me == 15)
            def _():
                eright_m[s] = esend[s, 1, 1]

            @pl.when(me == 16)
            def _():
                eleft_m[s] = esend[s, 0, 1]

    def edges_wait_near(s):
        left, right, _, _ = edge_copies(s)
        near_wait(left, right)

    def edges_wait_far(s):
        _, _, right_m, left_m = edge_copies(s)
        pl.when(not_15)(right_m.wait)
        pl.when(not_16)(left_m.wait)

    def edges_store(s, half, value):
        esend[s, 0, half] = value[0:16].astype(BF16)
        esend[s, 1, half] = value[16:32].astype(BF16)

    def halo(s, half, slot, mirrored):
        parts = [eright[s, half], eleft[s, half]]
        if mirrored:
            parts += [eright_m[s], eleft_m[s]]
        return dot(jnp.concatenate(parts, axis=0), place[slot, 0:16 * len(parts)], TN)

    def panel(step, g):
        src, dst = ((h0_hbm.at[g + 6], rc0.at[g]), (dzs1.at[g], rc2.at[g]), (dzs0.at[g], rc3.at[g]))[step]
        return copy(src, dst, psend.at[step, g], precv.at[step, g], to_mirror)

    for g in (0, 1):
        panel(0, g).start()

    def shifted(value, tail, sign):
        length = value.shape[1]
        whole = jnp.concatenate([value.astype(BF16), tail.astype(BF16)], axis=1)
        parts = []
        for k in range(5):
            shift = (sign * (2 - k)) % (length + 128)
            parts.append((whole if shift == 0 else pltpu.roll(whole, shift, 1))[:, :length])
        return jnp.concatenate(parts, axis=0)

    rev[...] = reversal(256)
    for i in range(6):
        pick0[i] = edge_pick(i, 256)
        pick1[i] = edge_pick(i, 128)
        place[i] = halo_place(i)

    def inverse_of(total):
        return lax.rsqrt(jnp.sum(total, axis=0, keepdims=True) / CHANNELS + 1e-06)

    def inverse_copy(b):
        src, dst = ((iv0s, iv0r), (iv1s, iv1r))[b]
        return copy(src, dst, ivsem.at[b], ivrsem.at[b], to_mirror)

    def normed(acts, inverse, column, length):
        return ((acts.astype(F32) * inverse) * wide(column, length)).astype(BF16)

    def norm(block, acts, inverse, length, target, pick, s):
        for half in (1, 0):
            def body(i, edge):
                g = half * 6 + i
                value = normed(acts[g], inverse, gcol[block * 12 + g], length)
                target[g] = value
                return edge + dot(pick[i], value, NT)
            edges_store(s, half, run(0, 6, body, jnp.zeros((32, 128), F32), PER))

    h0_load.wait()
    total0 = run(0, 12, lambda g, t: t + fold(jnp.square(h0[g].astype(F32))), jnp.zeros((8, 256), F32), 12)
    inv0 = inverse_of(total0)
    iv0s[...] = jnp.broadcast_to(inv0, (8, 256))
    inverse_copy(0).start()
    norm(0, h0, inv0, 256, nb0, pick0, 0)
    edges_start(0)
    for g in (2, 3):
        panel(0, g).start()

    w_load.wait()

    @pl.loop(0, 12)
    def _(g):
        for b in range(2):
            for k in range(5):
                wtr[b, g, :, k * 128:(k + 1) * 128] = wt_in[b, g, :, k * 128:(k + 1) * 128].T

    edges_wait_near(0)
    for g in (4, 5):
        panel(0, g).start()

    def pooled0(g, stack, acts):
        act, slope = gelu_parts(dot(wt_in[0, g], stack))
        high, low = two_terms(acts.astype(F32) + act)
        return (dot(high, spread[...], NT) + dot(low, spread[...], NT)).astype(BF16), slope

    def conv0(g, value, tail):
        stack = shifted(value, tail, 1)
        s0[g] = stack
        pooled, slope = pooled0(g, stack, h0[g])
        gp0[g] = slope
        h1[g] = pooled
        return fold(jnp.square(pooled.astype(F32)))

    def hi0(i, t):
        g = i + 6
        return t + conv0(g, nb0[g], halo(0, 1, i, False))

    def lo0(g, t):
        panel(0, g).wait()
        theirs = normed(rc0[g], iv0r[0:1, :], gcol[6 + g], 256)
        turned = dot(theirs, rev[...])
        nrev[g] = turned.astype(BF16)
        t = t + conv0(g, nb0[g].astype(F32) + turned, halo(0, 0, g, True))
        tail = dot(jnp.concatenate([eleft_m[0], eright_m[0]], axis=0), place[g, 0:32], TN)
        rc1[g], _ = pooled0(g + 6, shifted(theirs, tail, 1), rc0[g])
        return t

    total1 = run(0, 6, hi0, jnp.zeros((8, 128), F32), PER)
    edges_wait_far(0)
    inverse_copy(0).wait()
    total1 = run(0, 6, lo0, total1, 6)
    inv1 = inverse_of(total1)
    iv1s[...] = jnp.broadcast_to(inv1, (8, 128))
    inverse_copy(1).start()
    norm(1, h1, inv1, 128, nb1, pick1, 1)
    edges_start(1)
    edges_wait_near(1)

    def conv1(g, slot, value, tail):
        stack = shifted(value, tail, 1)
        s1[g] = stack
        act, slope = gelu_parts(dot(wt_in[1, g], stack))
        high, low = two_terms(h1[g].astype(F32) + act)
        half_spread = spread[0:64, 0:128]
        lanes = slice(g * 128, (g + 1) * 128)
        secb[:, lanes] = (dot(half_spread, high, NT) + dot(half_spread, low, NT)).astype(BF16)
        dr = dot(cot[:, lanes], half_spread, TN)
        dr1[g] = dr
        dy = (dr * slope).astype(BF16)
        dyb1[g] = dy
        return dot(pick1[slot], dy, NT)

    def hi1(i, e):
        g = i + 6
        return e + conv1(g, i, nb1[g], halo(1, 1, i, False))

    def lo1(g, e):
        turned = dot(normed(rc1[g], iv1r[0:1, :], gcol[18 + g], 128), rev[0:128, 128:256])
        nrev1[g] = turned.astype(BF16)
        return e + conv1(g, g, nb1[g].astype(F32) + turned, halo(1, 0, g, True))

    def weight_grads(b, dyb, stacks, half):
        def body(i, c):
            g = half * 6 + i
            grad = dot(dyb[g], stacks[g], NT).astype(BF16)
            for j in range(8):
                piece = g * 8 + j
                block = piece // 3
                w[b, block // 16, (block // 4) % 4, block % 4, piece % 3] = grad[j * 16:(j + 1) * 16]
            return c
        run(0, 6, body, 0, PER)

    def spans(half):
        mid = 256 if half else 384
        return pl.ds(0, mid), pl.ds(mid, 640 - mid)

    def first(b, half):
        one, two = spans(half)
        cps = []
        for d in range(1, 4):
            cps.append(copy(w.at[b, half, (x + d) % 4, :, :, :, one], rr.at[b, half, d - 1, :, :, :, one],
                            ss1.at[b, half, 0, d - 1], rs1.at[b, half, 0, d - 1], at_x(d)))
            cps.append(copy(w.at[b, half, :, (y + d) % 4, :, :, two], rr.at[b, half, d - 1, :, :, :, two],
                            ss1.at[b, half, 1, d - 1], rs1.at[b, half, 1, d - 1], at_y(d)))
        return cps

    def second(b, half):
        one, two = spans(half)
        cps = []
        for d in range(1, 4):
            cps.append(copy(pp.at[b, half, (y + d) % 4, :, :, one], qq.at[b, half, d - 1, :, :, one],
                            ss2.at[b, half, 0, d - 1], rs2.at[b, half, 0, d - 1], at_y(d)))
            cps.append(copy(pp.at[b, half, (x + d) % 4, :, :, two], qq.at[b, half, d - 1, :, :, two],
                            ss2.at[b, half, 1, d - 1], rs2.at[b, half, 1, d - 1], at_x(d)))
        return cps

    def third(b):
        return copy(sab.at[b, 1 - z], tz.at[b], ss3.at[b], rs3.at[b], at_z())

    def add_first(b, half):
        one, two = spans(half)
        for cp in first(b, half):
            cp.wait()

        @pl.loop(0, 4)
        def _(k):
            a = w[b, half, x, k, :, :, one].astype(F32)
            c = w[b, half, k, y, :, :, two].astype(F32)
            for d in range(3):
                a += rr[b, half, d, k, :, :, one].astype(F32)
                c += rr[b, half, d, k, :, :, two].astype(F32)
            pp[b, half, k, :, :, one] = a.astype(BF16)
            pp[b, half, k, :, :, two] = c.astype(BF16)
        for cp in second(b, half):
            cp.start()

    def add_second(b, half):
        one, two = spans(half)
        for cp in second(b, half):
            cp.wait()
        a = pp[b, half, y, :, :, one].astype(F32)
        c = pp[b, half, x, :, :, two].astype(F32)
        for d in range(3):
            a += qq[b, half, d, :, :, one].astype(F32)
            c += qq[b, half, d, :, :, two].astype(F32)
        sab[b, half, :, :, one] = a.astype(BF16)
        sab[b, half, :, :, two] = c.astype(BF16)
        pl.when(z != half)(third(b).start)

    def grads_out(b, dyb, stacks, half):
        weight_grads(b, dyb, stacks, half)
        for cp in first(b, half):
            cp.start()

    edges_store(2, 1, run(0, 6, hi1, jnp.zeros((32, 128), F32), 6))
    grads_out(1, dyb1, s1, 1)
    edges_wait_far(1)
    inverse_copy(1).wait()
    edges_store(2, 0, run(0, 6, lo1, jnp.zeros((32, 128), F32), 6))
    edges_start(2)
    sec_store = pltpu.make_async_copy(secb, sec_hbm, lsem.at[2])
    sec_store.start()
    grads_out(1, dyb1, s1, 0)
    edges_wait_near(2)

    def back(b, g, slot, half, s, dyb, length):
        return dot(wtr[b, g], shifted(dyb[g], halo(s, half, slot, False), -1)).astype(BF16)

    def scaled_sum(dn, xhat, row, length):
        weighted = dn * xhat
        column = jnp.sum(weighted, axis=1, keepdims=True)
        return fold(weighted * wide(gcol[row], length)), as_row(column)

    def lo1_back(g, c):
        q, theirs = c
        dz = back(1, g, g, 0, 2, dyb1, 128)
        dzs1[g] = dz
        panel(1, g).start()
        dn = dz.astype(F32)
        dn1[g] = dn
        part = fold(dn * (h1[g].astype(F32) * inv1) * gcol[12 + g])
        return q + part, theirs + fold(dn * nrev1[g].astype(F32))

    zero = jnp.zeros((8, 128), F32)
    q1, theirs1 = run(0, 6, lo1_back, (zero, zero), PER)
    high, low = two_terms(jnp.broadcast_to(jnp.sum(theirs1, axis=0, keepdims=True), (16, 128)))
    flip = rev[0:128, 128:256]
    qs[...] = dot(high, flip) + dot(low, flip)
    q_copy = copy(qs, qr, qsem.at[0], qrsem.at[0], to_mirror)
    q_copy.start()

    def hi1_own(g, q):
        dn = back(1, g, g - 6, 1, 2, dyb1, 128).astype(F32)
        dn1[g] = dn
        return q + fold(dn * (h1[g].astype(F32) * inv1) * gcol[12 + g])

    q1 = run(6, 12, hi1_own, q1, PER)
    add_first(1, 1)
    q_copy.wait()
    mean1 = (jnp.sum(q1, axis=0, keepdims=True) + qr[0:1, :]) / CHANNELS

    def grad_mid(half):
        def step(i, e):
            g = half * 6 + i
            dn = dn1[g]
            xhat = h1[g].astype(F32) * inv1
            if half:
                panel(1, i).wait()
                dn = dn + dot(rc2[i], rev[0:128, 128:256])
                dn1[g] = dn
            dh = (dn * gcol[12 + g] - xhat * mean1) * inv1 + dr1[g]
            high, low = two_terms(dh)
            dr = dot(high, spread[...]) + dot(low, spread[...])
            dr0[g] = dr
            dy = (dr * gp0[g]).astype(BF16)
            dyb0[g] = dy
            return e + dot(pick0[i], dy, NT)
        edges_store(3, half, run(0, 6, step, jnp.zeros((32, 128), F32), 6))
        half_start(3, half)
        grads_out(0, dyb0, s0, half)

    grad_mid(0)
    add_first(1, 0)
    grad_mid(1)

    def gains1(g, c):
        dgb[pl.ds(12 + g, 1), :] = as_row(jnp.sum(dn1[g] * (h1[g].astype(F32) * inv1), axis=1, keepdims=True))
        return c

    run(0, 12, gains1, 0, PER)
    half_wait(3, 0)

    def lo0_back(g, q):
        dz = back(0, g, g, 0, 3, dyb0, 256)
        dzs0[g] = dz
        panel(2, g).start()
        dn = dz.astype(F32)
        dn0[g] = dn
        part, row = scaled_sum(dn, h0[g].astype(F32) * inv0, g, 256)
        dgb[pl.ds(g, 1), :] = row
        column = jnp.sum(dn * nrev[g].astype(F32), axis=1, keepdims=True) / gcol[6 + g]
        dgb[pl.ds(6 + g, 1), :] = as_row(column)
        return q + part

    q0 = run(0, 6, lo0_back, jnp.zeros((8, 256), F32), PER)

    half_wait(3, 1)

    def hi0_own(g, c):
        dn = back(0, g, g - 6, 1, 3, dyb0, 256).astype(F32)
        dn0[g] = dn
        column = jnp.sum(dn * (h0[g].astype(F32) * inv0), axis=1, keepdims=True)
        dgb[pl.ds(g, 1), :] += as_row(column)
        return c

    run(6, 12, hi0_own, 0, PER)

    gbuf[0] = dgb[...]
    gx = [copy(gbuf.at[0], g1.at[d - 1], sg.at[0, d - 1], rg.at[0, d - 1], at_x(d)) for d in range(1, 4)]
    gy = [copy(gbuf.at[1], g2.at[d - 1], sg.at[1, d - 1], rg.at[1, d - 1], at_y(d)) for d in range(1, 4)]
    gz = copy(gbuf.at[2], g3, sg.at[2, 0], rg.at[2, 0], at_z())
    for cp in gx:
        cp.start()
    add_second(1, 1)
    add_second(1, 0)
    add_first(0, 0)
    for cp in gx:
        cp.wait()
    gbuf[1] = gbuf[0] + g1[0] + g1[1] + g1[2]
    for cp in gy:
        cp.start()
    add_first(0, 1)
    add_second(0, 0)
    for cp in gy:
        cp.wait()
    gbuf[2] = gbuf[1] + g2[0] + g2[1] + g2[2]
    gz.start()

    add_second(0, 1)
    gz.wait()
    total_g = gbuf[2] + g3[...]
    square = jnp.sum(total_g * total_g) * (1.0 / 32.0)
    for b in (1, 0):
        third(b).wait()
        full = sab[b, z].astype(F32) + tz[b].astype(F32)
        out[b] = full
        square += jnp.sum(full * full)
    sq[0] = jnp.full((8, 128), square, F32)
    near = [copy(sq.at[0], sq1.at[d - 1], sn.at[0], rn.at[0], at_plane(d)) for d in range(1, 16)]
    for cp in near:
        cp.start()

    def hi0_back(i, q):
        g = i + 6
        panel(2, i).wait()
        dn = dn0[g] + dot(rc3[i], rev[...])
        dn0[g] = dn
        xhat = h0[g].astype(F32) * inv0
        return q + fold(dn * xhat * wide(gcol[g], 256))

    q0 = run(0, 6, hi0_back, q0, 6)
    mean0 = jnp.sum(q0, axis=0, keepdims=True) / CHANNELS

    def finish(g, c):
        xhat = h0[g].astype(F32) * inv0
        igb[g] = ((dn0[g] * wide(gcol[g], 256) - xhat * mean0) * inv0 + dr0[g]).astype(BF16)
        return c

    run(0, 12, finish, 0, PER)
    ig_store = pltpu.make_async_copy(igb, ig_hbm, lsem.at[3])
    ig_store.start()
    copy(sq1, sq1, sn.at[0], rn.at[0], to_mirror).wait()
    sq[1] = sq[0] + jnp.sum(sq1[...], axis=0)
    far = [copy(sq.at[1], sq2.at[d - 1], sn.at[1], rn.at[1], at_line(d)) for d in range(1, 16)]
    for cp in far:
        cp.start()
    copy(sq2, sq2, sn.at[1], rn.at[1], to_mirror).wait()
    total = sq[1] + jnp.sum(sq2[...], axis=0)
    factor = jnp.minimum(1.0, lax.rsqrt(total / COUNT + 1e-06))[0:1, 0:1]
    for b in range(2):
        out[b] = out[b] * factor
    gfull[...] = total_g * factor
    start = me * 48
    for b in range(2):
        row = b * 12 + start // 128
        pair = jnp.concatenate([gfull[pl.ds(row, 1), :], gfull[pl.ds(row + 1, 1), :]], axis=1)
        pair = pltpu.roll(jnp.broadcast_to(pair, (8, 256)), (256 - start % 128) % 256, 1)
        gout[b:b + 1, :] = pair[0:1, 0:48]
    sec_store.wait()
    ig_store.wait()


def hand_on(*refs):
    count = len(refs) // 2
    for source, target in zip(refs[:count], refs[count:]):
        target[...] = source[...]


def local(section_input, out_cotangent, conv_weight, norm_gain):
    h0 = section_input.reshape(12, 128, 256)
    cot = out_cotangent[0].T
    weights = conv_weight.reshape(2, 12, 128, 640)
    gain = norm_gain[0]
    dma = pltpu.SemaphoreType.DMA

    def vm(shape, kind=BF16):
        return pltpu.VMEM(shape, kind)

    hbm = pl.BlockSpec(memory_space=pl.ANY)
    vmem = pl.BlockSpec(memory_space=pltpu.VMEM)
    second, grad_in, wshare, gshare = pl.pallas_call(
        kernel,
        out_shape=(
            jax.ShapeDtypeStruct((64, 1536), BF16),
            jax.ShapeDtypeStruct((12, 128, 256), BF16),
            jax.ShapeDtypeStruct((2, 3, 16, 640), F32),
            jax.ShapeDtypeStruct((2, 48), F32),
        ),
        in_specs=[hbm, vmem, hbm, vmem],
        out_specs=[hbm, hbm, vmem, vmem],
        scratch_shapes=[
            vm((12, 128, 256)), vm((2, 12, 128, 640)), vm((64, 1536)), vm((12, 128, 256)),
            vm((256, 256)), vm((128, 256)), vm((6, 32, 256)), vm((6, 32, 128)), vm((6, 64, 128)),
            vm((8, 256), F32), vm((8, 128), F32), vm((8, 256), F32), vm((8, 128), F32), vm((32, 128), F32),
            vm((24, 128, 128), F32), vm((2, 12, 128, 640)),
            vm((12, 128, 256)), vm((12, 128, 128)), vm((12, 128, 128)),
            vm((12, 640, 256)), vm((12, 640, 128)),
            vm((12, 128, 256), F32), vm((12, 128, 256), F32), vm((12, 128, 128), F32),
            vm((12, 128, 256)), vm((12, 128, 128)),
            vm((12, 128, 256), F32), vm((12, 128, 128), F32),
            vm((6, 128, 256)), vm((6, 128, 128)), vm((6, 128, 256)),
            vm((6, 128, 256)), vm((6, 128, 128)), vm((6, 128, 128)), vm((6, 128, 256)),
            vm((4, 2, 2, 16, 128)), vm((4, 2, 16, 128)), vm((4, 2, 16, 128)),
            vm((2, 16, 128)), vm((2, 16, 128)), vm((32, 128), F32),
            vm((2, 2, 4, 4, 3, 16, 640)), vm((2, 2, 3, 4, 3, 16, 640)),
            vm((2, 2, 4, 3, 16, 640)), vm((2, 2, 3, 3, 16, 640)),
            vm((2, 2, 3, 16, 640)), vm((2, 3, 16, 640)),
            vm((6, 128, 128)), vm((16, 128), F32), vm((16, 128), F32),
            vm((3, 32, 128), F32), vm((3, 32, 128), F32), vm((3, 32, 128), F32), vm((32, 128), F32),
            vm((2, 8, 128), F32), vm((15, 8, 128), F32), vm((15, 8, 128), F32),
            dma((3, 6)), dma((3, 6)), dma((4, 4)), dma((4, 4)), dma((2,)), dma((2,)), dma((4,)), dma((1,)), dma((1,)),
            dma((2, 2, 2, 3)), dma((2, 2, 2, 3)), dma((2, 2, 2, 3)), dma((2, 2, 2, 3)), dma((2,)), dma((2,)),
            dma((3, 3)), dma((3, 3)), dma((2,)), dma((2,)),
        ],
        compiler_params=pltpu.CompilerParams(
            collective_id=0, has_side_effects=True, vmem_limit_bytes=56 << 20),
        name="tower",
    )(h0, cot, weights, gain)
    second, grad_in, wshare, gshare = pl.pallas_call(
        hand_on,
        out_shape=[jax.ShapeDtypeStruct(a.shape, a.dtype) for a in (second, grad_in, wshare, gshare)],
        in_specs=[vmem] * 4,
        out_specs=[vmem] * 4,
        name="hand_on",
    )(second, grad_in, wshare, gshare)
    return (
        second.T[None],
        grad_in.reshape(1, 1536, 256),
        wshare.reshape(1, 2, 48, 640),
        gshare[None],
    )


def solution(mesh):
    placed = (
        P("section", None, "ctx"),
        P("section", None, "ctx"),
        P("section", None, None, None),
        P("section", None, None),
    )
    return jax.shard_map(
        local,
        mesh=mesh,
        in_specs=placed,
        out_specs=(
            P("section", None, "ctx"),
            P("section", None, "ctx"),
            P("section", None, "ctx", None),
            P("section", None, "ctx"),
        ),
        check_vma=False,
    )
```

```python
import jax
import jax.numpy as jnp
from jax import lax
from jax.experimental import pallas as pl
from jax.experimental.pallas import tpu as pltpu
from jax.sharding import PartitionSpec as P

MESH = pl.DeviceIdType.MESH
F32 = jnp.float32
BF16 = jnp.bfloat16
COUNT = 15753216.0
CHANNELS = 1536.0
PER = 6
NT = (((1,), (1,)), ((), ()))
TN = (((0,), (0,)), ((), ()))


def iota(shape, dim):
    return lax.broadcasted_iota(jnp.int32, shape, dim)


def dot(a, b, dims=(((1,), (0,)), ((), ()))):
    return lax.dot_general(a, b, dims, preferred_element_type=F32)


def two_terms(a):
    high = a.astype(BF16)
    return high, (a - high.astype(F32)).astype(BF16)


def reversal(length):
    shape = (length, length)
    return jnp.where(iota(shape, 0) + iota(shape, 1) == length - 1, 1.0, 0.0).astype(BF16)


def spreading(length):
    shape = (length // 2, length)
    return jnp.where(iota(shape, 0) == iota(shape, 1) // 2, 0.5, 0.0).astype(BF16)


def edge_pick(slot, length):
    shape = (32, length)
    row = iota(shape, 0)
    j = row % 16 - 2 * slot
    target = j + jnp.where(row >= 16, length - 2, 0)
    hit = jnp.logical_and(jnp.logical_and(j >= 0, j < 2), iota(shape, 1) == target)
    return jnp.where(hit, 1.0, 0.0).astype(BF16)


def halo_place(slot):
    shape = (64, 128)
    row = iota(shape, 0)
    block = row // 16
    j = row % 16 - 2 * slot
    straight = jnp.where(block == 0, j, 126 + j)
    turned = jnp.where(block == 2, 1 - j, 127 - j)
    target = jnp.where(block < 2, straight, turned)
    hit = jnp.logical_and(jnp.logical_and(j >= 0, j < 2), iota(shape, 1) == target)
    return jnp.where(hit, 1.0, 0.0).astype(BF16)


def wide(column, length):
    return column if length == 128 else jnp.concatenate([column] * (length // 128), axis=1)


def run(low, high, body, carry, per):
    if per >= high - low:
        for i in range(low, high):
            carry = body(i, carry)
        return carry

    def several(k, c):
        for u in range(per):
            c = body(low + k * per + u, c)
        return c
    return lax.fori_loop(0, (high - low) // per, several, carry)


def as_row(column):
    shape = (128, 128)
    return jnp.sum(jnp.where(iota(shape, 0) == iota(shape, 1), column, 0.0), axis=0, keepdims=True)


def fold(value):
    rows, length = value.shape
    return jnp.sum(value.reshape(rows // 8, 8, length), axis=0)


def gelu_parts(y):
    c0 = 0.7978845608028654
    square = y * y
    t = jnp.tanh(c0 * (y + 0.044715 * (square * y)))
    cdf = 0.5 * (1.0 + t)
    slope = cdf + 0.5 * y * (1.0 - t * t) * (c0 * (1.0 + 0.134145 * square))
    return y * cdf, slope


def kernel(h0_hbm, cot, wt_hbm, gain, sec_hbm, ig_hbm, out, gout,
           h0, wt_in, secb, igb, rev, spread, pick0, pick1, place, iv0s, iv1s, iv0r, iv1r, gfull,
           gcol, wtr, nb0, nb1, h1, s0, s1, gp0, dr0, dr1, dyb0, dyb1, dn0, dn1, dzs0, dzs1, nrev,
           rc0, rc1, rc2, rc3, esend, eright, eleft, eright_m, eleft_m, dgb,
           w, rr, pp, qq, sab, tz, nrev1, qs, qr, gbuf, g1, g2, g3, sq, sq1, sq2,
           psend, precv, esem, ersem, ivsem, ivrsem, lsem, qsem, qrsem,
           ss1, rs1, ss2, rs2, ss3, rs3, sg, rg, sn, rn):
    sec = lax.axis_index("section")
    me = lax.axis_index("ctx")
    z = me // 16
    x = (me // 4) % 4
    y = me % 4
    plane = me % 16
    line = sec * 2 + z
    has_left = me > 0
    has_right = me < 31
    not_15 = jnp.logical_and(has_right, me != 15)
    not_16 = jnp.logical_and(has_left, me != 16)

    def ctx(index):
        return {"section": sec, "ctx": index}

    def at_x(d):
        return ctx(z * 16 + ((x + d) % 4) * 4 + y)

    def at_y(d):
        return ctx(z * 16 + x * 4 + (y + d) % 4)

    def at_z():
        return ctx((1 - z) * 16 + plane)

    def at_plane(d):
        return ctx(z * 16 + (plane + d) % 16)

    def at_line(d):
        other = (line + d) % 16
        return {"section": other // 2, "ctx": (other % 2) * 16 + plane}

    to_mirror = ctx(31 - me)
    to_left = ctx((me + 31) % 32)
    to_right = ctx((me + 1) % 32)
    to_right_m = ctx((62 - me) % 32)
    to_left_m = ctx((32 - me) % 32)

    def copy(src, dst, send, recv, device):
        return pltpu.make_async_remote_copy(
            src_ref=src, dst_ref=dst, send_sem=send, recv_sem=recv,
            device_id=device, device_id_type=MESH)

    eright[...] = jnp.zeros_like(eright)
    eleft[...] = jnp.zeros_like(eleft)
    eright_m[...] = jnp.zeros_like(eright_m)
    eleft_m[...] = jnp.zeros_like(eleft_m)
    dgb[...] = jnp.zeros_like(dgb)

    barrier = pltpu.get_barrier_semaphore()

    def greet(device):
        pl.semaphore_signal(barrier, inc=1, device_id=device, device_id_type=MESH)

    greet(to_mirror)

    @pl.when(not_15)
    def _():
        greet(to_right_m)

    @pl.when(not_16)
    def _():
        greet(to_left_m)

    for d in (8, 7, 9, 6, 10, 5, 11, 4, 12, 3, 13, 2, 14, 1, 15):
        greet(at_line(d))

    @pl.when(has_left)
    def _():
        greet(to_left)

    @pl.when(has_right)
    def _():
        greet(to_right)

    for d in range(1, 16):
        greet(at_plane(d))

    h0_load = pltpu.make_async_copy(h0_hbm, h0, lsem.at[0])
    w_load = pltpu.make_async_copy(wt_hbm, wt_in, lsem.at[1])
    h0_load.start()
    w_load.start()

    for b in range(2):
        value = jnp.broadcast_to(gain[b:b + 1, :], (16, 1536))
        top = value.astype(BF16).astype(F32)
        middle = (value - top).astype(BF16).astype(F32)
        rest = value - top - middle
        row = iota((16, 1536), 0)
        terms = jnp.where(row == 0, top, jnp.where(row == 1, middle, jnp.where(row == 2, rest, 0.0)))
        terms = terms.astype(BF16)
        ones = jnp.ones((16, 128), BF16)
        for g in range(12):
            gcol[b * 12 + g] = dot(terms[:, g * 128:(g + 1) * 128], ones, TN)
    spread[0:128] = spreading(256)
    spread[128:256] = spreading(256)

    pl.semaphore_wait(
        barrier, 31 + has_left.astype(jnp.int32) + has_right.astype(jnp.int32)
        + not_15.astype(jnp.int32) + not_16.astype(jnp.int32))

    def half_copies(s, half):
        left = copy(esend.at[s, 0, half], eright.at[s, half], esem.at[s, 2 * half], ersem.at[s, 2 * half], to_left)
        right = copy(esend.at[s, 1, half], eleft.at[s, half],
                     esem.at[s, 2 * half + 1], ersem.at[s, 2 * half + 1], to_right)
        return left, right

    def half_start(s, half):
        left, right = half_copies(s, half)
        pl.when(has_left)(left.start)
        pl.when(has_right)(right.start)

    def near_wait(left, right):
        pl.when(has_left)(left.wait_send)
        pl.when(has_right)(left.wait_recv)
        pl.when(has_right)(right.wait_send)
        pl.when(has_left)(right.wait_recv)

    def half_wait(s, half):
        near_wait(*half_copies(s, half))

    def edge_copies(s):
        left = copy(esend.at[s, 0], eright.at[s], esem.at[s, 0], ersem.at[s, 0], to_left)
        right = copy(esend.at[s, 1], eleft.at[s], esem.at[s, 1], ersem.at[s, 1], to_right)
        right_m = left_m = None
        if s < 2:
            right_m = copy(esend.at[s, 1, 1], eright_m.at[s], esem.at[s, 2], ersem.at[s, 2], to_right_m)
            left_m = copy(esend.at[s, 0, 1], eleft_m.at[s], esem.at[s, 3], ersem.at[s, 3], to_left_m)
        return left, right, right_m, left_m

    def edges_start(s):
        left, right, right_m, left_m = edge_copies(s)
        pl.when(has_left)(left.start)
        pl.when(has_right)(right.start)
        if s < 2:
            pl.when(not_15)(right_m.start)
            pl.when(not_16)(left_m.start)

            @pl.when(me == 15)
            def _():
                eright_m[s] = esend[s, 1, 1]

            @pl.when(me == 16)
            def _():
                eleft_m[s] = esend[s, 0, 1]

    def edges_wait_near(s):
        left, right, _, _ = edge_copies(s)
        near_wait(left, right)

    def edges_wait_far(s):
        _, _, right_m, left_m = edge_copies(s)
        pl.when(not_15)(right_m.wait)
        pl.when(not_16)(left_m.wait)

    def edges_store(s, half, value):
        esend[s, 0, half] = value[0:16].astype(BF16)
        esend[s, 1, half] = value[16:32].astype(BF16)

    def halo(s, half, slot, mirrored):
        parts = [eright[s, half], eleft[s, half]]
        if mirrored:
            parts += [eright_m[s], eleft_m[s]]
        return dot(jnp.concatenate(parts, axis=0), place[slot, 0:16 * len(parts)], TN)

    def panel(step, g):
        src, dst = ((h0_hbm.at[g + 6], rc0.at[g]), (dzs1.at[g], rc2.at[g]), (dzs0.at[g], rc3.at[g]))[step]
        return copy(src, dst, psend.at[step, g], precv.at[step, g], to_mirror)

    for g in (0, 1):
        panel(0, g).start()

    def shifted(value, tail, sign):
        length = value.shape[1]
        whole = jnp.concatenate([value.astype(BF16), tail.astype(BF16)], axis=1)
        parts = []
        for k in range(5):
            shift = (sign * (2 - k)) % (length + 128)
            parts.append((whole if shift == 0 else pltpu.roll(whole, shift, 1))[:, :length])
        return jnp.concatenate(parts, axis=0)

    rev[...] = reversal(256)
    for i in range(6):
        pick0[i] = edge_pick(i, 256)
        pick1[i] = edge_pick(i, 128)
        place[i] = halo_place(i)

    def inverse_of(total):
        return lax.rsqrt(jnp.sum(total, axis=0, keepdims=True) / CHANNELS + 1e-06)

    def inverse_copy(b):
        src, dst = ((iv0s, iv0r), (iv1s, iv1r))[b]
        return copy(src, dst, ivsem.at[b], ivrsem.at[b], to_mirror)

    def normed(acts, inverse, column, length):
        return ((acts.astype(F32) * inverse) * wide(column, length)).astype(BF16)

    def norm(block, acts, inverse, length, target, pick, s):
        for half in (1, 0):
            def body(i, edge):
                g = half * 6 + i
                value = normed(acts[g], inverse, gcol[block * 12 + g], length)
                target[g] = value
                return edge + dot(pick[i], value, NT) if length == 256 else edge
            edge = run(0, 6, body, jnp.zeros((32, 128), F32), PER)
            edges_store(s, half, edge if length == 256 else paired_edges(target, half))

    def paired_edges(source, half):
        edge = jnp.zeros((32, 128), F32)
        for i in (0, 2, 4):
            g = half * 6 + i
            edge += dot(jnp.concatenate([pick1[i], pick1[i + 1]], axis=1),
                        jnp.concatenate([source[g], source[g + 1]], axis=1), NT)
        return edge

    h0_load.wait()
    total0 = run(0, 12, lambda g, t: t + fold(jnp.square(h0[g].astype(F32))), jnp.zeros((8, 256), F32), 12)
    inv0 = inverse_of(total0)
    iv0s[...] = jnp.broadcast_to(inv0, (8, 256))
    inverse_copy(0).start()
    norm(0, h0, inv0, 256, nb0, pick0, 0)
    edges_start(0)
    for g in (2, 3):
        panel(0, g).start()

    w_load.wait()

    @pl.loop(0, 12)
    def _(g):
        for b in range(2):
            for k in range(5):
                wtr[b, g, :, k * 128:(k + 1) * 128] = wt_in[b, g, :, k * 128:(k + 1) * 128].T

    dr1[...] = dot(cot[...], spread[0:64, 0:128], TN).reshape(12, 128, 128)
    edges_wait_near(0)
    for g in (4, 5):
        panel(0, g).start()

    def pooled0(g, stack, acts):
        act, slope = gelu_parts(dot(wt_in[0, g], stack))
        high, low = two_terms(acts.astype(F32) + act)
        return (dot(high, spread[0:128], NT) + dot(low, spread[0:128], NT)).astype(BF16), slope

    def conv0(g, value, tail):
        stack = shifted(value, tail, 1)
        s0[g] = stack
        pooled, slope = pooled0(g, stack, h0[g])
        gp0[g] = slope
        h1[g] = pooled
        return fold(jnp.square(pooled.astype(F32)))

    def hi0(i, t):
        g = i + 6
        return t + conv0(g, nb0[g], halo(0, 1, i, False))

    def lo0(g, t):
        panel(0, g).wait()
        panel(0, g + 1).wait()
        both = jnp.concatenate(
            [normed(rc0[k], iv0r[0:1, :], gcol[6 + k], 256) for k in (g, g + 1)], axis=0)
        turned = dot(both, rev[...])
        for k in (g, g + 1):
            rows = slice((k - g) * 128, (k - g + 1) * 128)
            nrev[k] = turned[rows].astype(BF16)
            t = t + conv0(k, nb0[k].astype(F32) + turned[rows], halo(0, 0, k, True))
            tail = dot(jnp.concatenate([eleft_m[0], eright_m[0]], axis=0), place[k, 0:32], TN)
            rc1[k], _ = pooled0(k + 6, shifted(both[rows], tail, 1), rc0[k])
        return t

    total1 = run(0, 6, hi0, jnp.zeros((8, 128), F32), PER)
    edges_wait_far(0)
    inverse_copy(0).wait()
    for g in (0, 2, 4):
        total1 = lo0(g, total1)
    inv1 = inverse_of(total1)
    iv1s[...] = jnp.broadcast_to(inv1, (8, 128))
    inverse_copy(1).start()
    norm(1, h1, inv1, 128, nb1, pick1, 1)
    edges_start(1)
    edges_wait_near(1)

    def conv1(g, value, tail):
        stack = shifted(value, tail, 1)
        s1[g] = stack
        act, slope = gelu_parts(dot(wt_in[1, g], stack))
        terms = jnp.concatenate(two_terms(h1[g].astype(F32) + act), axis=1)
        half_spread = spread[0:64, 0:128]
        pooled = dot(jnp.concatenate([half_spread, half_spread], axis=1), terms, NT)
        secb[:, g * 128:(g + 1) * 128] = pooled.astype(BF16)
        dyb1[g] = (dr1[g] * slope).astype(BF16)

    def weight_grads(b, dyb, stacks, half):
        def body(i, c):
            g = half * 6 + i
            grad = dot(dyb[g], stacks[g], NT).astype(BF16)
            for j in range(8):
                piece = g * 8 + j
                block = piece // 3
                w[b, block // 16, (block // 4) % 4, block % 4, piece % 3] = grad[j * 16:(j + 1) * 16]
            return c
        run(0, 6, body, 0, PER)

    def spans(half):
        mid = 256 if half else 384
        return pl.ds(0, mid), pl.ds(mid, 640 - mid)

    def first(b, half):
        one, two = spans(half)
        cps = []
        for d in range(1, 4):
            cps.append(copy(w.at[b, half, (x + d) % 4, :, :, :, one], rr.at[b, half, d - 1, :, :, :, one],
                            ss1.at[b, half, 0, d - 1], rs1.at[b, half, 0, d - 1], at_x(d)))
            cps.append(copy(w.at[b, half, :, (y + d) % 4, :, :, two], rr.at[b, half, d - 1, :, :, :, two],
                            ss1.at[b, half, 1, d - 1], rs1.at[b, half, 1, d - 1], at_y(d)))
        return cps

    def second(b, half):
        one, two = spans(half)
        cps = []
        for d in range(1, 4):
            cps.append(copy(pp.at[b, half, (y + d) % 4, :, :, one], qq.at[b, half, d - 1, :, :, one],
                            ss2.at[b, half, 0, d - 1], rs2.at[b, half, 0, d - 1], at_y(d)))
            cps.append(copy(pp.at[b, half, (x + d) % 4, :, :, two], qq.at[b, half, d - 1, :, :, two],
                            ss2.at[b, half, 1, d - 1], rs2.at[b, half, 1, d - 1], at_x(d)))
        return cps

    def third(b):
        return copy(sab.at[b, 1 - z], tz.at[b], ss3.at[b], rs3.at[b], at_z())

    def add_first(b, half):
        one, two = spans(half)
        for cp in first(b, half):
            cp.wait()

        @pl.loop(0, 4)
        def _(k):
            a = w[b, half, x, k, :, :, one].astype(F32)
            c = w[b, half, k, y, :, :, two].astype(F32)
            for d in range(3):
                a += rr[b, half, d, k, :, :, one].astype(F32)
                c += rr[b, half, d, k, :, :, two].astype(F32)
            pp[b, half, k, :, :, one] = a.astype(BF16)
            pp[b, half, k, :, :, two] = c.astype(BF16)
        for cp in second(b, half):
            cp.start()

    def add_second(b, half):
        one, two = spans(half)
        for cp in second(b, half):
            cp.wait()
        a = pp[b, half, y, :, :, one].astype(F32)
        c = pp[b, half, x, :, :, two].astype(F32)
        for d in range(3):
            a += qq[b, half, d, :, :, one].astype(F32)
            c += qq[b, half, d, :, :, two].astype(F32)
        sab[b, half, :, :, one] = a.astype(BF16)
        sab[b, half, :, :, two] = c.astype(BF16)
        pl.when(z != half)(third(b).start)

    def grads_out(b, dyb, stacks, half):
        weight_grads(b, dyb, stacks, half)
        for cp in first(b, half):
            cp.start()

    for i in range(6):
        conv1(i + 6, nb1[i + 6], halo(1, 1, i, False))
    edges_store(2, 1, paired_edges(dyb1, 1))
    distant = jnp.logical_or(me == 15, me == 16)

    grads_out(1, dyb1, s1, 1)

    edges_wait_far(1)
    inverse_copy(1).wait()
    theirs = jnp.concatenate([normed(rc1[g], iv1r[0:1, :], gcol[18 + g], 128) for g in range(6)], axis=0)
    turned = dot(theirs, rev[0:128, 128:256])
    for g in range(6):
        part = turned[g * 128:(g + 1) * 128]
        nrev1[g] = part.astype(BF16)
        conv1(g, nb1[g].astype(F32) + part, halo(1, 0, g, True))
    edges_store(2, 0, paired_edges(dyb1, 0))
    edges_start(2)
    sec_store = pltpu.make_async_copy(secb, sec_hbm, lsem.at[2])
    sec_store.start()
    grads_out(1, dyb1, s1, 0)

    edges_wait_near(2)

    def back(b, g, slot, half, s, dyb, length):
        return dot(wtr[b, g], shifted(dyb[g], halo(s, half, slot, False), -1)).astype(BF16)

    def scaled_sum(dn, xhat, row, length):
        weighted = dn * xhat
        column = jnp.sum(weighted, axis=1, keepdims=True)
        return fold(weighted * wide(gcol[row], length)), as_row(column)

    def lo1_back(g, c):
        q, theirs = c
        dz = back(1, g, g, 0, 2, dyb1, 128)
        dzs1[g] = dz
        dn = dz.astype(F32)
        dn1[g] = dn
        part = fold(dn * (h1[g].astype(F32) * inv1) * gcol[12 + g])
        return q + part, theirs + fold(dn * nrev1[g].astype(F32))

    zero = jnp.zeros((8, 128), F32)
    q1, theirs1 = run(0, 6, lo1_back, (zero, zero), PER)
    high, low = two_terms(jnp.broadcast_to(jnp.sum(theirs1, axis=0, keepdims=True), (16, 128)))
    flip = rev[0:128, 128:256]
    qs[...] = dot(high, flip) + dot(low, flip)
    q_copy = copy(qs, qr, qsem.at[0], qrsem.at[0], to_mirror)
    q_copy.start()
    for g in range(3):
        panel(1, g).start()

    def hi1_own(g, q):
        dn = back(1, g, g - 6, 1, 2, dyb1, 128).astype(F32)
        dn1[g] = dn
        return q + fold(dn * (h1[g].astype(F32) * inv1) * gcol[12 + g])

    q1 = run(6, 12, hi1_own, q1, PER)
    for g in range(3, 6):
        panel(1, g).start()
    add_first(1, 1)
    q_copy.wait()
    mean1 = (jnp.sum(q1, axis=0, keepdims=True) + qr[0:1, :]) / CHANNELS

    def grad_mid(half):
        if half:
            for i in range(6):
                panel(1, i).wait()
            turned = dot(rc2[...].reshape(768, 128), rev[0:128, 128:256])

        def step(i, e):
            g = half * 6 + i
            dn = dn1[g]
            xhat = h1[g].astype(F32) * inv1
            if half:
                dn = dn + turned[i * 128:(i + 1) * 128]
                dn1[g] = dn
            dh = (dn * gcol[12 + g] - xhat * mean1) * inv1 + dr1[g]
            dr = dot(jnp.concatenate(two_terms(dh), axis=1), spread[...])
            dr0[g] = dr
            dy = (dr * gp0[g]).astype(BF16)
            dyb0[g] = dy
            return e + dot(pick0[i], dy, NT)
        edges_store(3, half, run(0, 6, step, jnp.zeros((32, 128), F32), 6))
        half_start(3, half)
        grads_out(0, dyb0, s0, half)

    grad_mid(0)
    add_first(1, 0)
    grad_mid(1)

    def gains1(g, c):
        dgb[pl.ds(12 + g, 1), :] = as_row(jnp.sum(dn1[g] * (h1[g].astype(F32) * inv1), axis=1, keepdims=True))
        return c

    run(0, 12, gains1, 0, PER)
    half_wait(3, 0)

    def lo0_back(g, q):
        dz = back(0, g, g, 0, 3, dyb0, 256)
        dzs0[g] = dz
        if g < 2:
            panel(2, g).start()
        dn = dz.astype(F32)
        dn0[g] = dn
        part, row = scaled_sum(dn, h0[g].astype(F32) * inv0, g, 256)
        dgb[pl.ds(g, 1), :] = row
        column = jnp.sum(dn * nrev[g].astype(F32), axis=1, keepdims=True) / gcol[6 + g]
        dgb[pl.ds(6 + g, 1), :] = as_row(column)
        return q + part

    q0 = run(0, 6, lo0_back, jnp.zeros((8, 256), F32), PER)

    half_wait(3, 1)

    def hi0_own(g, c):
        dn = back(0, g, g - 6, 1, 3, dyb0, 256).astype(F32)
        dn0[g] = dn
        column = jnp.sum(dn * (h0[g].astype(F32) * inv0), axis=1, keepdims=True)
        dgb[pl.ds(g, 1), :] += as_row(column)
        return c

    run(6, 12, hi0_own, 0, PER)

    for g in (2, 3):
        panel(2, g).start()
    gbuf[0] = dgb[...]
    gx = [copy(gbuf.at[0], g1.at[d - 1], sg.at[0, d - 1], rg.at[0, d - 1], at_x(d)) for d in range(1, 4)]
    gy = [copy(gbuf.at[1], g2.at[d - 1], sg.at[1, d - 1], rg.at[1, d - 1], at_y(d)) for d in range(1, 4)]
    gz = copy(gbuf.at[2], g3, sg.at[2, 0], rg.at[2, 0], at_z())
    for cp in gx:
        cp.start()
    add_second(1, 1)
    add_second(1, 0)
    add_first(0, 0)
    for g in (4, 5):
        panel(2, g).start()
    for cp in gx:
        cp.wait()
    gbuf[1] = gbuf[0] + g1[0] + g1[1] + g1[2]
    for cp in gy:
        cp.start()
    add_first(0, 1)
    add_second(0, 0)
    for cp in gy:
        cp.wait()
    gbuf[2] = gbuf[1] + g2[0] + g2[1] + g2[2]
    gz.start()

    add_second(0, 1)
    gz.wait()
    total_g = gbuf[2] + g3[...]
    square = jnp.sum(total_g * total_g) * (1.0 / 32.0)
    for b in (1, 0):
        third(b).wait()
        full = sab[b, z].astype(F32) + tz[b].astype(F32)
        out[b] = full
        square += jnp.sum(full * full)
    sq[0] = jnp.full((8, 128), square, F32)
    near = [copy(sq.at[0], sq1.at[d - 1], sn.at[0], rn.at[0], at_plane(d)) for d in range(1, 16)]
    for cp in near:
        cp.start()

    copy(sq1, sq1, sn.at[0], rn.at[0], to_mirror).wait()
    sq[1] = sq[0] + jnp.sum(sq1[...], axis=0)
    far = [copy(sq.at[1], sq2.at[d - 1], sn.at[1], rn.at[1], at_line(d)) for d in range(1, 16)]
    for cp in far:
        cp.start()
    def hi0_back(i, q):
        g = i + 6
        panel(2, i).wait()
        dn = dn0[g] + dot(rc3[i], rev[...])
        dn0[g] = dn
        xhat = h0[g].astype(F32) * inv0
        return q + fold(dn * xhat * wide(gcol[g], 256))

    q0 = run(0, 6, hi0_back, q0, 6)
    mean0 = jnp.sum(q0, axis=0, keepdims=True) / CHANNELS

    def finish(g, c):
        xhat = h0[g].astype(F32) * inv0
        igb[g] = ((dn0[g] * wide(gcol[g], 256) - xhat * mean0) * inv0 + dr0[g]).astype(BF16)
        return c

    run(0, 12, finish, 0, PER)
    ig_store = pltpu.make_async_copy(igb, ig_hbm, lsem.at[3])
    ig_store.start()
    copy(sq2, sq2, sn.at[1], rn.at[1], to_mirror).wait()
    total = sq[1] + jnp.sum(sq2[...], axis=0)
    factor = jnp.minimum(1.0, lax.rsqrt(total / COUNT + 1e-06))[0:1, 0:1]
    for b in range(2):
        out[b] = out[b] * factor
    gfull[...] = total_g * factor
    start = me * 48
    for b in range(2):
        row = b * 12 + start // 128
        pair = jnp.concatenate([gfull[pl.ds(row, 1), :], gfull[pl.ds(row + 1, 1), :]], axis=1)
        pair = pltpu.roll(jnp.broadcast_to(pair, (8, 256)), (256 - start % 128) % 256, 1)
        gout[b:b + 1, :] = pair[0:1, 0:48]
    sec_store.wait()
    ig_store.wait()


def hand_on(*refs):
    count = len(refs) // 2
    for source, target in zip(refs[:count], refs[count:]):
        target[...] = source[...]


def local(section_input, out_cotangent, conv_weight, norm_gain):
    h0 = section_input.reshape(12, 128, 256)
    cot = out_cotangent[0].T
    weights = conv_weight.reshape(2, 12, 128, 640)
    gain = norm_gain[0]
    dma = pltpu.SemaphoreType.DMA

    def vm(shape, kind=BF16):
        return pltpu.VMEM(shape, kind)

    hbm = pl.BlockSpec(memory_space=pl.ANY)
    vmem = pl.BlockSpec(memory_space=pltpu.VMEM)
    second, grad_in, wshare, gshare = pl.pallas_call(
        kernel,
        out_shape=(
            jax.ShapeDtypeStruct((64, 1536), BF16),
            jax.ShapeDtypeStruct((12, 128, 256), BF16),
            jax.ShapeDtypeStruct((2, 3, 16, 640), F32),
            jax.ShapeDtypeStruct((2, 48), F32),
        ),
        in_specs=[hbm, vmem, hbm, vmem],
        out_specs=[hbm, hbm, vmem, vmem],
        scratch_shapes=[
            vm((12, 128, 256)), vm((2, 12, 128, 640)), vm((64, 1536)), vm((12, 128, 256)),
            vm((256, 256)), vm((256, 256)), vm((6, 32, 256)), vm((6, 32, 128)), vm((6, 64, 128)),
            vm((8, 256), F32), vm((8, 128), F32), vm((8, 256), F32), vm((8, 128), F32), vm((32, 128), F32),
            vm((24, 128, 128), F32), vm((2, 12, 128, 640)),
            vm((12, 128, 256)), vm((12, 128, 128)), vm((12, 128, 128)),
            vm((12, 640, 256)), vm((12, 640, 128)),
            vm((12, 128, 256), F32), vm((12, 128, 256), F32), vm((12, 128, 128), F32),
            vm((12, 128, 256)), vm((12, 128, 128)),
            vm((12, 128, 256), F32), vm((12, 128, 128), F32),
            vm((6, 128, 256)), vm((6, 128, 128)), vm((6, 128, 256)),
            vm((6, 128, 256)), vm((6, 128, 128)), vm((6, 128, 128)), vm((6, 128, 256)),
            vm((4, 2, 2, 16, 128)), vm((4, 2, 16, 128)), vm((4, 2, 16, 128)),
            vm((2, 16, 128)), vm((2, 16, 128)), vm((32, 128), F32),
            vm((2, 2, 4, 4, 3, 16, 640)), vm((2, 2, 3, 4, 3, 16, 640)),
            vm((2, 2, 4, 3, 16, 640)), vm((2, 2, 3, 3, 16, 640)),
            vm((2, 2, 3, 16, 640)), vm((2, 3, 16, 640)),
            vm((6, 128, 128)), vm((16, 128), F32), vm((16, 128), F32),
            vm((3, 32, 128), F32), vm((3, 32, 128), F32), vm((3, 32, 128), F32), vm((32, 128), F32),
            vm((2, 8, 128), F32), vm((15, 8, 128), F32), vm((15, 8, 128), F32),
            dma((3, 6)), dma((3, 6)), dma((4, 4)), dma((4, 4)), dma((2,)), dma((2,)), dma((4,)), dma((1,)), dma((1,)),
            dma((2, 2, 2, 3)), dma((2, 2, 2, 3)), dma((2, 2, 2, 3)), dma((2, 2, 2, 3)), dma((2,)), dma((2,)),
            dma((3, 3)), dma((3, 3)), dma((2,)), dma((2,)),
        ],
        compiler_params=pltpu.CompilerParams(
            collective_id=0, has_side_effects=True, vmem_limit_bytes=56 << 20),
        name="tower",
    )(h0, cot, weights, gain)
    second, grad_in, wshare, gshare = pl.pallas_call(
        hand_on,
        out_shape=[jax.ShapeDtypeStruct(a.shape, a.dtype) for a in (second, grad_in, wshare, gshare)],
        in_specs=[vmem] * 4,
        out_specs=[vmem] * 4,
        name="hand_on",
    )(second, grad_in, wshare, gshare)
    return (
        second.T[None],
        grad_in.reshape(1, 1536, 256),
        wshare.reshape(1, 2, 48, 640),
        gshare[None],
    )


def solution(mesh):
    placed = (
        P("section", None, "ctx"),
        P("section", None, "ctx"),
        P("section", None, None, None),
        P("section", None, None),
    )
    return jax.shard_map(
        local,
        mesh=mesh,
        in_specs=placed,
        out_specs=(
            P("section", None, "ctx"),
            P("section", None, "ctx"),
            P("section", None, "ctx", None),
            P("section", None, "ctx"),
        ),
        check_vma=False,
    )
```

```python
import jax
import jax.numpy as jnp
from jax import lax
from jax.experimental import pallas as pl
from jax.experimental.pallas import tpu as pltpu
from jax.sharding import PartitionSpec as P

MESH = pl.DeviceIdType.MESH
F32 = jnp.float32
BF16 = jnp.bfloat16
COUNT = 15753216.0
CHANNELS = 1536.0
PER = 6
NT = (((1,), (1,)), ((), ()))
TN = (((0,), (0,)), ((), ()))


def iota(shape, dim):
    return lax.broadcasted_iota(jnp.int32, shape, dim)


def dot(a, b, dims=(((1,), (0,)), ((), ()))):
    return lax.dot_general(a, b, dims, preferred_element_type=F32)


def two_terms(a):
    high = a.astype(BF16)
    return high, (a - high.astype(F32)).astype(BF16)


def reversal(length):
    shape = (length, length)
    return jnp.where(iota(shape, 0) + iota(shape, 1) == length - 1, 1.0, 0.0).astype(BF16)


def spreading(length):
    shape = (length // 2, length)
    return jnp.where(iota(shape, 0) == iota(shape, 1) // 2, 0.5, 0.0).astype(BF16)


def edge_pick(slot, length):
    shape = (32, length)
    row = iota(shape, 0)
    j = row % 16 - 2 * slot
    target = j + jnp.where(row >= 16, length - 2, 0)
    hit = jnp.logical_and(jnp.logical_and(j >= 0, j < 2), iota(shape, 1) == target)
    return jnp.where(hit, 1.0, 0.0).astype(BF16)


def halo_place(slot):
    shape = (64, 128)
    row = iota(shape, 0)
    block = row // 16
    j = row % 16 - 2 * slot
    straight = jnp.where(block == 0, j, 126 + j)
    turned = jnp.where(block == 2, 1 - j, 127 - j)
    target = jnp.where(block < 2, straight, turned)
    hit = jnp.logical_and(jnp.logical_and(j >= 0, j < 2), iota(shape, 1) == target)
    return jnp.where(hit, 1.0, 0.0).astype(BF16)


def wide(column, length):
    return column if length == 128 else jnp.concatenate([column] * (length // 128), axis=1)


def run(low, high, body, carry, per):
    if per >= high - low:
        for i in range(low, high):
            carry = body(i, carry)
        return carry

    def several(k, c):
        for u in range(per):
            c = body(low + k * per + u, c)
        return c
    return lax.fori_loop(0, (high - low) // per, several, carry)


def as_row(column):
    shape = (128, 128)
    return jnp.sum(jnp.where(iota(shape, 0) == iota(shape, 1), column, 0.0), axis=0, keepdims=True)


def fold(value):
    rows, length = value.shape
    return jnp.sum(value.reshape(rows // 8, 8, length), axis=0)


def gelu_parts(y):
    c0 = 0.7978845608028654
    square = y * y
    t = jnp.tanh(c0 * (y + 0.044715 * (square * y)))
    cdf = 0.5 * (1.0 + t)
    slope = cdf + 0.5 * y * (1.0 - t * t) * (c0 * (1.0 + 0.134145 * square))
    return y * cdf, slope


def kernel(h0_hbm, cot, wt_hbm, gain, sec_hbm, ig_hbm, out, gout,
           h0, wt_in, secb, igb, rev, spread, pick0, pick1, place, iv0s, iv1s, iv0r, iv1r, gfull,
           gcol, wtr, nb0, nb1, h1, s0, s1, gp0, dr0, dr1, dyb0, dyb1, dn0, dn1, dzs0, dzs1, nrev,
           rc0, rc1, rc2, rc3, esend, eright, eleft, eright_m, eleft_m, dgb,
           w, rr, pp, qq, sab, tz, nrev1, qs, qr, gbuf, g1, g2, g3, sq, sq1, sq2,
           psend, precv, esem, ersem, ivsem, ivrsem, lsem, qsem, qrsem,
           ss1, rs1, ss2, rs2, ss3, rs3, sg, rg, sn, rn):
    sec = lax.axis_index("section")
    me = lax.axis_index("ctx")
    z = me // 16
    x = (me // 4) % 4
    y = me % 4
    plane = me % 16
    line = sec * 2 + z
    has_left = me > 0
    has_right = me < 31
    not_15 = jnp.logical_and(has_right, me != 15)
    not_16 = jnp.logical_and(has_left, me != 16)

    def ctx(index):
        return {"section": sec, "ctx": index}

    def at_x(d):
        return ctx(z * 16 + ((x + d) % 4) * 4 + y)

    def at_y(d):
        return ctx(z * 16 + x * 4 + (y + d) % 4)

    def at_z():
        return ctx((1 - z) * 16 + plane)

    def at_plane(d):
        return ctx(z * 16 + (plane + d) % 16)

    def at_line(d):
        other = (line + d) % 16
        return {"section": other // 2, "ctx": (other % 2) * 16 + plane}

    to_mirror = ctx(31 - me)
    to_left = ctx((me + 31) % 32)
    to_right = ctx((me + 1) % 32)
    to_right_m = ctx((62 - me) % 32)
    to_left_m = ctx((32 - me) % 32)

    def copy(src, dst, send, recv, device):
        return pltpu.make_async_remote_copy(
            src_ref=src, dst_ref=dst, send_sem=send, recv_sem=recv,
            device_id=device, device_id_type=MESH)

    eright[...] = jnp.zeros_like(eright)
    eleft[...] = jnp.zeros_like(eleft)
    eright_m[...] = jnp.zeros_like(eright_m)
    eleft_m[...] = jnp.zeros_like(eleft_m)
    dgb[...] = jnp.zeros_like(dgb)

    barrier = pltpu.get_barrier_semaphore()

    def greet(device):
        pl.semaphore_signal(barrier, inc=1, device_id=device, device_id_type=MESH)

    greet(to_mirror)

    @pl.when(not_15)
    def _():
        greet(to_right_m)

    @pl.when(not_16)
    def _():
        greet(to_left_m)

    for d in (8, 7, 9, 6, 10, 5, 11, 4, 12, 3, 13, 2, 14, 1, 15):
        greet(at_line(d))

    @pl.when(has_left)
    def _():
        greet(to_left)

    @pl.when(has_right)
    def _():
        greet(to_right)

    for d in range(1, 16):
        greet(at_plane(d))

    h0_load = pltpu.make_async_copy(h0_hbm, h0, lsem.at[0])
    w_load = pltpu.make_async_copy(wt_hbm, wt_in, lsem.at[1])
    h0_load.start()
    w_load.start()

    for b in range(2):
        value = jnp.broadcast_to(gain[b:b + 1, :], (16, 1536))
        top = value.astype(BF16).astype(F32)
        middle = (value - top).astype(BF16).astype(F32)
        rest = value - top - middle
        row = iota((16, 1536), 0)
        terms = jnp.where(row == 0, top, jnp.where(row == 1, middle, jnp.where(row == 2, rest, 0.0)))
        terms = terms.astype(BF16)
        ones = jnp.ones((16, 128), BF16)
        for g in range(12):
            gcol[b * 12 + g] = dot(terms[:, g * 128:(g + 1) * 128], ones, TN)
    spread[0:128] = spreading(256)
    spread[128:256] = spreading(256)

    pl.semaphore_wait(
        barrier, 31 + has_left.astype(jnp.int32) + has_right.astype(jnp.int32)
        + not_15.astype(jnp.int32) + not_16.astype(jnp.int32))

    def half_copies(s, half):
        left = copy(esend.at[s, 0, half], eright.at[s, half], esem.at[s, 2 * half], ersem.at[s, 2 * half], to_left)
        right = copy(esend.at[s, 1, half], eleft.at[s, half],
                     esem.at[s, 2 * half + 1], ersem.at[s, 2 * half + 1], to_right)
        return left, right

    def half_start(s, half):
        left, right = half_copies(s, half)
        pl.when(has_left)(left.start)
        pl.when(has_right)(right.start)

    def near_wait(left, right):
        pl.when(has_left)(left.wait_send)
        pl.when(has_right)(left.wait_recv)
        pl.when(has_right)(right.wait_send)
        pl.when(has_left)(right.wait_recv)

    def half_wait(s, half):
        near_wait(*half_copies(s, half))

    def edge_copies(s):
        left = copy(esend.at[s, 0], eright.at[s], esem.at[s, 0], ersem.at[s, 0], to_left)
        right = copy(esend.at[s, 1], eleft.at[s], esem.at[s, 1], ersem.at[s, 1], to_right)
        right_m = left_m = None
        if s < 2:
            right_m = copy(esend.at[s, 1, 1], eright_m.at[s], esem.at[s, 2], ersem.at[s, 2], to_right_m)
            left_m = copy(esend.at[s, 0, 1], eleft_m.at[s], esem.at[s, 3], ersem.at[s, 3], to_left_m)
        return left, right, right_m, left_m

    def edges_start(s):
        left, right, right_m, left_m = edge_copies(s)
        pl.when(has_left)(left.start)
        pl.when(has_right)(right.start)
        if s < 2:
            pl.when(not_15)(right_m.start)
            pl.when(not_16)(left_m.start)

            @pl.when(me == 15)
            def _():
                eright_m[s] = esend[s, 1, 1]

            @pl.when(me == 16)
            def _():
                eleft_m[s] = esend[s, 0, 1]

    def edges_wait_near(s):
        left, right, _, _ = edge_copies(s)
        near_wait(left, right)

    def edges_wait_far(s):
        _, _, right_m, left_m = edge_copies(s)
        pl.when(not_15)(right_m.wait)
        pl.when(not_16)(left_m.wait)

    def edges_store(s, half, value):
        esend[s, 0, half] = value[0:16].astype(BF16)
        esend[s, 1, half] = value[16:32].astype(BF16)

    def halo(s, half, slot, mirrored):
        parts = [eright[s, half], eleft[s, half]]
        if mirrored:
            parts += [eright_m[s], eleft_m[s]]
        return dot(jnp.concatenate(parts, axis=0), place[slot, 0:16 * len(parts)], TN)

    def panel(step, g):
        src, dst = ((h0_hbm.at[g + 6], rc0.at[g]), (dzs1.at[g], rc2.at[g]), (dzs0.at[g], rc3.at[g]))[step]
        return copy(src, dst, psend.at[step, g], precv.at[step, g], to_mirror)

    for g in (0, 1):
        panel(0, g).start()

    def shifted(value, tail, sign):
        length = value.shape[1]
        whole = jnp.concatenate([value.astype(BF16), tail.astype(BF16)], axis=1)
        parts = []
        for k in range(5):
            shift = (sign * (2 - k)) % (length + 128)
            parts.append((whole if shift == 0 else pltpu.roll(whole, shift, 1))[:, :length])
        return jnp.concatenate(parts, axis=0)

    rev[...] = reversal(256)
    for i in range(6):
        pick0[i] = edge_pick(i, 256)
        pick1[i] = edge_pick(i, 128)
        place[i] = halo_place(i)

    def inverse_of(total):
        return lax.rsqrt(jnp.sum(total, axis=0, keepdims=True) / CHANNELS + 1e-06)

    def inverse_copy(b):
        src, dst = ((iv0s, iv0r), (iv1s, iv1r))[b]
        return copy(src, dst, ivsem.at[b], ivrsem.at[b], to_mirror)

    def normed(acts, inverse, column, length):
        return ((acts.astype(F32) * inverse) * wide(column, length)).astype(BF16)

    def norm(block, acts, inverse, length, target, pick, s):
        for half in (1, 0):
            def body(i, edge):
                g = half * 6 + i
                value = normed(acts[g], inverse, gcol[block * 12 + g], length)
                target[g] = value
                return edge + dot(pick[i], value, NT) if length == 256 else edge
            edge = run(0, 6, body, jnp.zeros((32, 128), F32), PER)
            edges_store(s, half, edge if length == 256 else paired_edges(target, half))

    def paired_edges(source, half):
        edge = jnp.zeros((32, 128), F32)
        for i in (0, 2, 4):
            g = half * 6 + i
            edge += dot(jnp.concatenate([pick1[i], pick1[i + 1]], axis=1),
                        jnp.concatenate([source[g], source[g + 1]], axis=1), NT)
        return edge

    h0_load.wait()
    total0 = run(0, 12, lambda g, t: t + fold(jnp.square(h0[g].astype(F32))), jnp.zeros((8, 256), F32), 12)
    inv0 = inverse_of(total0)
    iv0s[...] = jnp.broadcast_to(inv0, (8, 256))
    inverse_copy(0).start()
    norm(0, h0, inv0, 256, nb0, pick0, 0)
    edges_start(0)
    for g in (2, 3):
        panel(0, g).start()

    w_load.wait()

    @pl.loop(0, 12)
    def _(g):
        for b in range(2):
            for k in range(5):
                wtr[b, g, :, k * 128:(k + 1) * 128] = wt_in[b, g, :, k * 128:(k + 1) * 128].T

    dr1[...] = dot(cot[...], spread[0:64, 0:128], TN).reshape(12, 128, 128)
    edges_wait_near(0)
    for g in (4, 5):
        panel(0, g).start()

    def pooled0(g, stack, acts):
        act, slope = gelu_parts(dot(wt_in[0, g], stack))
        high, low = two_terms(acts.astype(F32) + act)
        return (dot(high, spread[0:128], NT) + dot(low, spread[0:128], NT)).astype(BF16), slope

    def conv0(g, value, tail):
        stack = shifted(value, tail, 1)
        s0[g] = stack
        pooled, slope = pooled0(g, stack, h0[g])
        gp0[g] = slope
        h1[g] = pooled
        return fold(jnp.square(pooled.astype(F32)))

    def hi0(i, t):
        g = i + 6
        return t + conv0(g, nb0[g], halo(0, 1, i, False))

    def lo0(g, t):
        panel(0, g).wait()
        panel(0, g + 1).wait()
        both = jnp.concatenate(
            [normed(rc0[k], iv0r[0:1, :], gcol[6 + k], 256) for k in (g, g + 1)], axis=0)
        turned = dot(both, rev[...])
        for k in (g, g + 1):
            rows = slice((k - g) * 128, (k - g + 1) * 128)
            nrev[k] = turned[rows].astype(BF16)
            t = t + conv0(k, nb0[k].astype(F32) + turned[rows], halo(0, 0, k, True))
            tail = dot(jnp.concatenate([eleft_m[0], eright_m[0]], axis=0), place[k, 0:32], TN)
            rc1[k], _ = pooled0(k + 6, shifted(both[rows], tail, 1), rc0[k])
        return t

    total1 = run(0, 6, hi0, jnp.zeros((8, 128), F32), PER)
    edges_wait_far(0)
    inverse_copy(0).wait()
    for g in (0, 2, 4):
        total1 = lo0(g, total1)
    inv1 = inverse_of(total1)
    iv1s[...] = jnp.broadcast_to(inv1, (8, 128))
    inverse_copy(1).start()
    norm(1, h1, inv1, 128, nb1, pick1, 1)
    edges_start(1)
    edges_wait_near(1)

    def conv1(g, value, tail):
        stack = shifted(value, tail, 1)
        s1[g] = stack
        act, slope = gelu_parts(dot(wt_in[1, g], stack))
        terms = jnp.concatenate(two_terms(h1[g].astype(F32) + act), axis=1)
        half_spread = spread[0:64, 0:128]
        pooled = dot(jnp.concatenate([half_spread, half_spread], axis=1), terms, NT)
        secb[:, g * 128:(g + 1) * 128] = pooled.astype(BF16)
        dyb1[g] = (dr1[g] * slope).astype(BF16)

    def weight_grads(b, dyb, stacks, half):
        def body(i, c):
            g = half * 6 + i
            grad = dot(dyb[g], stacks[g], NT).astype(BF16)
            for j in range(8):
                piece = g * 8 + j
                block = piece // 3
                w[b, block // 16, (block // 4) % 4, block % 4, piece % 3] = grad[j * 16:(j + 1) * 16]
            return c
        run(0, 6, body, 0, PER)

    def spans(half):
        mid = 256 if half else 384
        return pl.ds(0, mid), pl.ds(mid, 640 - mid)

    def first(b, half):
        one, two = spans(half)
        cps = []
        for d in range(1, 4):
            cps.append(copy(w.at[b, half, (x + d) % 4, :, :, :, one], rr.at[b, half, d - 1, :, :, :, one],
                            ss1.at[b, half, 0, d - 1], rs1.at[b, half, 0, d - 1], at_x(d)))
            cps.append(copy(w.at[b, half, :, (y + d) % 4, :, :, two], rr.at[b, half, d - 1, :, :, :, two],
                            ss1.at[b, half, 1, d - 1], rs1.at[b, half, 1, d - 1], at_y(d)))
        return cps

    def second(b, half):
        one, two = spans(half)
        cps = []
        for d in range(1, 4):
            cps.append(copy(pp.at[b, half, (y + d) % 4, :, :, one], qq.at[b, half, d - 1, :, :, one],
                            ss2.at[b, half, 0, d - 1], rs2.at[b, half, 0, d - 1], at_y(d)))
            cps.append(copy(pp.at[b, half, (x + d) % 4, :, :, two], qq.at[b, half, d - 1, :, :, two],
                            ss2.at[b, half, 1, d - 1], rs2.at[b, half, 1, d - 1], at_x(d)))
        return cps

    def third(b):
        return copy(sab.at[b, 1 - z], tz.at[b], ss3.at[b], rs3.at[b], at_z())

    def add_first(b, half):
        one, two = spans(half)
        for cp in first(b, half):
            cp.wait()

        @pl.loop(0, 4)
        def _(k):
            a = w[b, half, x, k, :, :, one].astype(F32)
            c = w[b, half, k, y, :, :, two].astype(F32)
            for d in range(3):
                a += rr[b, half, d, k, :, :, one].astype(F32)
                c += rr[b, half, d, k, :, :, two].astype(F32)
            pp[b, half, k, :, :, one] = a.astype(BF16)
            pp[b, half, k, :, :, two] = c.astype(BF16)
        for cp in second(b, half):
            cp.start()

    def add_second(b, half):
        one, two = spans(half)
        for cp in second(b, half):
            cp.wait()
        a = pp[b, half, y, :, :, one].astype(F32)
        c = pp[b, half, x, :, :, two].astype(F32)
        for d in range(3):
            a += qq[b, half, d, :, :, one].astype(F32)
            c += qq[b, half, d, :, :, two].astype(F32)
        sab[b, half, :, :, one] = a.astype(BF16)
        sab[b, half, :, :, two] = c.astype(BF16)
        pl.when(z != half)(third(b).start)

    def grads_out(b, dyb, stacks, half):
        weight_grads(b, dyb, stacks, half)
        for cp in first(b, half):
            cp.start()

    for i in range(6):
        conv1(i + 6, nb1[i + 6], halo(1, 1, i, False))
    edges_store(2, 1, paired_edges(dyb1, 1))
    distant = jnp.logical_or(me == 15, me == 16)

    weight_grads(1, dyb1, s1, 1)

    edges_wait_far(1)
    inverse_copy(1).wait()
    for cp in first(1, 1):
        cp.start()
    theirs = jnp.concatenate([normed(rc1[g], iv1r[0:1, :], gcol[18 + g], 128) for g in range(6)], axis=0)
    turned = dot(theirs, rev[0:128, 128:256])
    for g in range(6):
        part = turned[g * 128:(g + 1) * 128]
        nrev1[g] = part.astype(BF16)
        conv1(g, nb1[g].astype(F32) + part, halo(1, 0, g, True))
    edges_store(2, 0, paired_edges(dyb1, 0))
    edges_start(2)
    sec_store = pltpu.make_async_copy(secb, sec_hbm, lsem.at[2])
    sec_store.start()
    grads_out(1, dyb1, s1, 0)

    edges_wait_near(2)

    def back(b, g, slot, half, s, dyb, length):
        return dot(wtr[b, g], shifted(dyb[g], halo(s, half, slot, False), -1)).astype(BF16)

    def scaled_sum(dn, xhat, row, length):
        weighted = dn * xhat
        column = jnp.sum(weighted, axis=1, keepdims=True)
        return fold(weighted * wide(gcol[row], length)), as_row(column)

    def lo1_back(g, c):
        q, theirs = c
        dz = back(1, g, g, 0, 2, dyb1, 128)
        dzs1[g] = dz
        dn = dz.astype(F32)
        dn1[g] = dn
        part = fold(dn * (h1[g].astype(F32) * inv1) * gcol[12 + g])
        return q + part, theirs + fold(dn * nrev1[g].astype(F32))

    zero = jnp.zeros((8, 128), F32)
    q1, theirs1 = run(0, 6, lo1_back, (zero, zero), PER)
    high, low = two_terms(jnp.broadcast_to(jnp.sum(theirs1, axis=0, keepdims=True), (16, 128)))
    flip = rev[0:128, 128:256]
    qs[...] = dot(high, flip) + dot(low, flip)
    q_copy = copy(qs, qr, qsem.at[0], qrsem.at[0], to_mirror)
    q_copy.start()
    for g in range(3):
        panel(1, g).start()

    def hi1_own(g, q):
        dn = back(1, g, g - 6, 1, 2, dyb1, 128).astype(F32)
        dn1[g] = dn
        return q + fold(dn * (h1[g].astype(F32) * inv1) * gcol[12 + g])

    q1 = run(6, 12, hi1_own, q1, PER)
    for g in range(3, 6):
        panel(1, g).start()
    add_first(1, 1)
    q_copy.wait()
    mean1 = (jnp.sum(q1, axis=0, keepdims=True) + qr[0:1, :]) / CHANNELS

    def grad_mid(half):
        if half:
            for i in range(6):
                panel(1, i).wait()
            turned = dot(rc2[...].reshape(768, 128), rev[0:128, 128:256])

        def step(i, e):
            g = half * 6 + i
            dn = dn1[g]
            xhat = h1[g].astype(F32) * inv1
            if half:
                dn = dn + turned[i * 128:(i + 1) * 128]
                dn1[g] = dn
            dh = (dn * gcol[12 + g] - xhat * mean1) * inv1 + dr1[g]
            dr = dot(jnp.concatenate(two_terms(dh), axis=1), spread[...])
            dr0[g] = dr
            dy = (dr * gp0[g]).astype(BF16)
            dyb0[g] = dy
            return e + dot(pick0[i], dy, NT)
        edges_store(3, half, run(0, 6, step, jnp.zeros((32, 128), F32), 6))
        half_start(3, half)
        grads_out(0, dyb0, s0, half)

    grad_mid(0)
    add_first(1, 0)
    grad_mid(1)

    def gains1(g, c):
        dgb[pl.ds(12 + g, 1), :] = as_row(jnp.sum(dn1[g] * (h1[g].astype(F32) * inv1), axis=1, keepdims=True))
        return c

    run(0, 12, gains1, 0, PER)
    half_wait(3, 0)

    def lo0_back(g, q):
        dz = back(0, g, g, 0, 3, dyb0, 256)
        dzs0[g] = dz
        if g < 2:
            panel(2, g).start()
        dn = dz.astype(F32)
        dn0[g] = dn
        part, row = scaled_sum(dn, h0[g].astype(F32) * inv0, g, 256)
        dgb[pl.ds(g, 1), :] = row
        column = jnp.sum(dn * nrev[g].astype(F32), axis=1, keepdims=True) / gcol[6 + g]
        dgb[pl.ds(6 + g, 1), :] = as_row(column)
        return q + part

    q0 = run(0, 6, lo0_back, jnp.zeros((8, 256), F32), PER)

    half_wait(3, 1)

    def hi0_own(g, c):
        dn = back(0, g, g - 6, 1, 3, dyb0, 256).astype(F32)
        dn0[g] = dn
        column = jnp.sum(dn * (h0[g].astype(F32) * inv0), axis=1, keepdims=True)
        dgb[pl.ds(g, 1), :] += as_row(column)
        return c

    run(6, 12, hi0_own, 0, PER)

    for g in (2, 3):
        panel(2, g).start()
    gbuf[0] = dgb[...]
    gx = [copy(gbuf.at[0], g1.at[d - 1], sg.at[0, d - 1], rg.at[0, d - 1], at_x(d)) for d in range(1, 4)]
    gy = [copy(gbuf.at[1], g2.at[d - 1], sg.at[1, d - 1], rg.at[1, d - 1], at_y(d)) for d in range(1, 4)]
    gz = copy(gbuf.at[2], g3, sg.at[2, 0], rg.at[2, 0], at_z())
    for cp in gx:
        cp.start()
    add_second(1, 1)
    add_second(1, 0)
    add_first(0, 0)
    for g in (4, 5):
        panel(2, g).start()
    for cp in gx:
        cp.wait()
    gbuf[1] = gbuf[0] + g1[0] + g1[1] + g1[2]
    for cp in gy:
        cp.start()
    add_first(0, 1)
    add_second(0, 0)
    for cp in gy:
        cp.wait()
    gbuf[2] = gbuf[1] + g2[0] + g2[1] + g2[2]
    gz.start()

    add_second(0, 1)
    gz.wait()
    total_g = gbuf[2] + g3[...]
    square = jnp.sum(total_g * total_g) * (1.0 / 32.0)
    for b in (1, 0):
        third(b).wait()
        full = sab[b, z].astype(F32) + tz[b].astype(F32)
        out[b] = full
        square += jnp.sum(full * full)
    sq[0] = jnp.full((8, 128), square, F32)
    near = [copy(sq.at[0], sq1.at[d - 1], sn.at[0], rn.at[0], at_plane(d)) for d in range(1, 16)]
    for cp in near:
        cp.start()

    copy(sq1, sq1, sn.at[0], rn.at[0], to_mirror).wait()
    sq[1] = sq[0] + jnp.sum(sq1[...], axis=0)
    far = [copy(sq.at[1], sq2.at[d - 1], sn.at[1], rn.at[1], at_line(d)) for d in range(1, 16)]
    for cp in far:
        cp.start()
    def hi0_back(i, q):
        g = i + 6
        panel(2, i).wait()
        dn = dn0[g] + dot(rc3[i], rev[...])
        dn0[g] = dn
        xhat = h0[g].astype(F32) * inv0
        return q + fold(dn * xhat * wide(gcol[g], 256))

    q0 = run(0, 6, hi0_back, q0, 6)
    mean0 = jnp.sum(q0, axis=0, keepdims=True) / CHANNELS

    def finish(g, c):
        xhat = h0[g].astype(F32) * inv0
        igb[g] = ((dn0[g] * wide(gcol[g], 256) - xhat * mean0) * inv0 + dr0[g]).astype(BF16)
        return c

    run(0, 12, finish, 0, PER)
    ig_store = pltpu.make_async_copy(igb, ig_hbm, lsem.at[3])
    ig_store.start()
    copy(sq2, sq2, sn.at[1], rn.at[1], to_mirror).wait()
    total = sq[1] + jnp.sum(sq2[...], axis=0)
    factor = jnp.minimum(1.0, lax.rsqrt(total / COUNT + 1e-06))[0:1, 0:1]
    for b in range(2):
        out[b] = out[b] * factor
    gfull[...] = total_g * factor
    start = me * 48
    for b in range(2):
        row = b * 12 + start // 128
        pair = jnp.concatenate([gfull[pl.ds(row, 1), :], gfull[pl.ds(row + 1, 1), :]], axis=1)
        pair = pltpu.roll(jnp.broadcast_to(pair, (8, 256)), (256 - start % 128) % 256, 1)
        gout[b:b + 1, :] = pair[0:1, 0:48]
    sec_store.wait()
    ig_store.wait()


def hand_on(*refs):
    count = len(refs) // 2
    for source, target in zip(refs[:count], refs[count:]):
        target[...] = source[...]


def local(section_input, out_cotangent, conv_weight, norm_gain):
    h0 = section_input.reshape(12, 128, 256)
    cot = out_cotangent[0].T
    weights = conv_weight.reshape(2, 12, 128, 640)
    gain = norm_gain[0]
    dma = pltpu.SemaphoreType.DMA

    def vm(shape, kind=BF16):
        return pltpu.VMEM(shape, kind)

    hbm = pl.BlockSpec(memory_space=pl.ANY)
    vmem = pl.BlockSpec(memory_space=pltpu.VMEM)
    second, grad_in, wshare, gshare = pl.pallas_call(
        kernel,
        out_shape=(
            jax.ShapeDtypeStruct((64, 1536), BF16),
            jax.ShapeDtypeStruct((12, 128, 256), BF16),
            jax.ShapeDtypeStruct((2, 3, 16, 640), F32),
            jax.ShapeDtypeStruct((2, 48), F32),
        ),
        in_specs=[hbm, vmem, hbm, vmem],
        out_specs=[hbm, hbm, vmem, vmem],
        scratch_shapes=[
            vm((12, 128, 256)), vm((2, 12, 128, 640)), vm((64, 1536)), vm((12, 128, 256)),
            vm((256, 256)), vm((256, 256)), vm((6, 32, 256)), vm((6, 32, 128)), vm((6, 64, 128)),
            vm((8, 256), F32), vm((8, 128), F32), vm((8, 256), F32), vm((8, 128), F32), vm((32, 128), F32),
            vm((24, 128, 128), F32), vm((2, 12, 128, 640)),
            vm((12, 128, 256)), vm((12, 128, 128)), vm((12, 128, 128)),
            vm((12, 640, 256)), vm((12, 640, 128)),
            vm((12, 128, 256), F32), vm((12, 128, 256), F32), vm((12, 128, 128), F32),
            vm((12, 128, 256)), vm((12, 128, 128)),
            vm((12, 128, 256), F32), vm((12, 128, 128), F32),
            vm((6, 128, 256)), vm((6, 128, 128)), vm((6, 128, 256)),
            vm((6, 128, 256)), vm((6, 128, 128)), vm((6, 128, 128)), vm((6, 128, 256)),
            vm((4, 2, 2, 16, 128)), vm((4, 2, 16, 128)), vm((4, 2, 16, 128)),
            vm((2, 16, 128)), vm((2, 16, 128)), vm((32, 128), F32),
            vm((2, 2, 4, 4, 3, 16, 640)), vm((2, 2, 3, 4, 3, 16, 640)),
            vm((2, 2, 4, 3, 16, 640)), vm((2, 2, 3, 3, 16, 640)),
            vm((2, 2, 3, 16, 640)), vm((2, 3, 16, 640)),
            vm((6, 128, 128)), vm((16, 128), F32), vm((16, 128), F32),
            vm((3, 32, 128), F32), vm((3, 32, 128), F32), vm((3, 32, 128), F32), vm((32, 128), F32),
            vm((2, 8, 128), F32), vm((15, 8, 128), F32), vm((15, 8, 128), F32),
            dma((3, 6)), dma((3, 6)), dma((4, 4)), dma((4, 4)), dma((2,)), dma((2,)), dma((4,)), dma((1,)), dma((1,)),
            dma((2, 2, 2, 3)), dma((2, 2, 2, 3)), dma((2, 2, 2, 3)), dma((2, 2, 2, 3)), dma((2,)), dma((2,)),
            dma((3, 3)), dma((3, 3)), dma((2,)), dma((2,)),
        ],
        compiler_params=pltpu.CompilerParams(
            collective_id=0, has_side_effects=True, vmem_limit_bytes=56 << 20),
        name="tower",
    )(h0, cot, weights, gain)
    second, grad_in, wshare, gshare = pl.pallas_call(
        hand_on,
        out_shape=[jax.ShapeDtypeStruct(a.shape, a.dtype) for a in (second, grad_in, wshare, gshare)],
        in_specs=[vmem] * 4,
        out_specs=[vmem] * 4,
        name="hand_on",
    )(second, grad_in, wshare, gshare)
    return (
        second.T[None],
        grad_in.reshape(1, 1536, 256),
        wshare.reshape(1, 2, 48, 640),
        gshare[None],
    )


def solution(mesh):
    placed = (
        P("section", None, "ctx"),
        P("section", None, "ctx"),
        P("section", None, None, None),
        P("section", None, None),
    )
    return jax.shard_map(
        local,
        mesh=mesh,
        in_specs=placed,
        out_specs=(
            P("section", None, "ctx"),
            P("section", None, "ctx"),
            P("section", None, "ctx", None),
            P("section", None, "ctx"),
        ),
        check_vma=False,
    )
```
